32 devices in a mesh: scen: 2 (over y), tm: 4 (over z), bus: 4 (over x, core).
Axes of the slice: x: 2, y: 2, z: 4, core: 2. Of those that a mesh axis runs over, the one named last changes fastest.
Arguments:
- gen_start: float32 [512, 2560], P(('scen', 'tm'), 'bus'), parts along dimension 0, may hold values from 0 to 1
- charge_start: float32 [512, 1024], P(('scen', 'tm'), 'bus'), parts along dimension 0, may hold values from -3 to 3
- load: bfloat16 [512, 17920], P(('scen', 'tm'), 'bus'), parts along dimension 0, may hold values from 0 to 0.19921875
- ptdf_tiles: bfloat16 [464, 128, 128], P('bus'), may hold values from -0.5 to 0.5
- tile_row: int32 [464], P('bus'), may hold values from 0 to 79
- tile_col: int32 [464], P('bus'), may hold values from 0 to 34
- gen_bus: int32 [2560], P('bus'), may hold values from 0 to 4479
- stor_bus: int32 [1024], P('bus'), may hold values from 0 to 4479
- gen_cost: float32 [2560], P('bus'), may hold values from 0 to 1
- gen_max: float32 [2560], P('bus'), may hold values from 0.5 to 3
- ramp_limit: float32 [2560], P('bus'), may hold values from 0.05 to 0.5
- stor_power: float32 [1024], P('bus'), may hold values from 0.3 to 2
- stor_loss: float32 [1024], P('bus'), may hold values from 0.02 to 0.3
- stor_cap: float32 [1024], P('bus'), may hold values from 0.5 to 3
- flow_limit: float32 [10240], replicated, may hold values from 0.5 to 2
Outputs:
- gen_next: float32 [512, 2560], P(('scen', 'tm'), 'bus'), parts along dimension 0
- charge_next: float32 [512, 1024], P(('scen', 'tm'), 'bus'), parts along dimension 0
- line_dual: float32 [512, 10240], P(('scen', 'tm'), 'bus'), parts along dimension 0
The draws below stay inside these ranges and needn't reach their ends.
There are 2 independent parts, one for each index of `scen`. The reference program is written for one: setup_inputs(seed, part) draws one part's arguments, and reference() takes and returns one part's arrays. A program takes and returns all parts, laid end to end along the dimension named above; an argument that names none is the same for every part. Nothing has to cross between parts.
Inputs may be any that keep to these rules, and one draw needn't show every extreme that they name: Stored tile k lies in line tile tile_row[k] of the 80; pairs of tile_row and tile_col may repeat, and repeated tiles add. Stored tile k covers the buses 128 * tile_col[k] to 128 * tile_col[k] + 127 of the block (k // 116). `gen_bus`: A bus index within the block of generator i, which is block i // 640. `stor_bus`: A bus index within the block of storage unit s, which is block s // 256.
All inputs are finite; a program needn't handle non-finite values.
Results may differ from the reference program's by a relative error of at most 0.028.
Values may be sent and summed in bfloat16 or wider, within the bound.
No kernel may reach another device: no remote copies, remote signals or barrier semaphores. Data moves between devices by JAX's collectives and lax.ppermute only.
A program may use at most 128 MiB of HBM per device.

```python
import math
import jax
import jax.numpy as jnp
from jax import lax

TILE = 128
LINES = 10240
LTILES = 80
BUS_DEV = 4480
CTILES = 35
NBUS = 17920
G_DEV = 640
NGEN = 2560
S_DEV = 256
NSTOR = 1024
KT = 116
TILES = 464
HOURS = 256
ITERS = 3
N_BUS = 4


def place_ends(result, own_key, least, top_value):
    dims = result.shape
    place = [jax.random.randint(jax.random.fold_in(own_key, axis), (), 0, dims[axis]) for axis in range(len(dims))]
    result = result.at[tuple(place)].set(least)
    longest = dims.index(max(dims))
    place[longest] = (place[longest] + 1) % dims[longest]
    return result.at[tuple(place)].set(top_value)


def block_scale(key, dims, cuts, least, largest):
    factor_of, own = 1.0, jax.random.fold_in(key, 6)
    for axis_at, blocks in cuts:
        heights = jnp.exp(jax.random.uniform(jax.random.fold_in(own, axis_at), (blocks,), jnp.float32, least / len(cuts), largest / len(cuts)))
        factor_of = factor_of * jnp.repeat(heights, dims[axis_at] // blocks).reshape([-1 if axis == axis_at else 1 for axis in range(len(dims))])
    return factor_of


def normal_values(stream_key, dims, spread, most, split=(), held_as=jnp.bfloat16):
    gain = block_scale(stream_key, dims, split, -0.22, 0.18) if split else 1.0
    array = jax.random.normal(stream_key, dims, jnp.float32) * spread * gain
    return jnp.minimum(jnp.maximum(array, -most), most).astype(held_as)


def setup_inputs(seed: int = 0, part: int = 0) -> dict:
    streams_of = jax.random.split(jax.random.key(seed), 16)
    part_splits = jax.random.split(jax.random.fold_in(streams_of[15], part), 16)
    gen_start = jnp.clip(1.0 * jax.random.uniform(part_splits[0], (HOURS, NGEN), jnp.float32) ** block_scale(part_splits[0], (HOURS, NGEN), ((0, 4), (1, 4)), -0.2, 0.2), 0.0, 1.0)
    charge_start = normal_values(part_splits[1], (HOURS, NSTOR), 0.5, 3.0, ((0, 4), (1, 4)), jnp.float32)
    load = jnp.clip(0.19921875 * jax.random.uniform(part_splits[2], (HOURS, NBUS), jnp.float32) ** block_scale(part_splits[2], (HOURS, NBUS), ((0, 4), (1, 4)), -0.2, 0.2), 0.0, 0.19921875).astype(jnp.bfloat16)
    ptdf_tiles = normal_values(streams_of[3], (TILES, TILE, TILE), (KT * N_BUS * TILE * (G_DEV + S_DEV) // (LTILES * BUS_DEV)) ** -0.5, 0.5, ((0, 4),))
    tile_row = place_ends(jax.random.randint(streams_of[4], (TILES,), 0, LTILES), jax.random.fold_in(streams_of[4], 1), 0, LTILES - 1).astype(jnp.int32)
    tile_col = place_ends(jax.random.randint(streams_of[5], (TILES,), 0, CTILES), jax.random.fold_in(streams_of[5], 1), 0, CTILES - 1).astype(jnp.int32)
    gen_bus = place_ends(jax.random.randint(streams_of[6], (NGEN,), 0, BUS_DEV), jax.random.fold_in(streams_of[6], 1), 0, BUS_DEV - 1).astype(jnp.int32)
    stor_bus = place_ends(jax.random.randint(streams_of[7], (NSTOR,), 0, BUS_DEV), jax.random.fold_in(streams_of[7], 1), 0, BUS_DEV - 1).astype(jnp.int32)
    gen_cost = jnp.clip(1.0 * jax.random.uniform(streams_of[8], (NGEN,), jnp.float32) ** block_scale(streams_of[8], (NGEN,), ((0, 4),), -0.2, 0.2), 0.0, 1.0)
    gen_max = jnp.clip(jnp.exp(math.log(3.0) - 1.7917595 * jax.random.uniform(streams_of[9], (NGEN,), jnp.float32) ** block_scale(streams_of[9], (NGEN,), ((0, 4),), -0.2, 0.2)), 0.5, 3.0)
    ramp_limit = jnp.clip(jnp.exp(math.log(0.5) - 2.3025851 * jax.random.uniform(streams_of[10], (NGEN,), jnp.float32) ** block_scale(streams_of[10], (NGEN,), ((0, 4),), -0.2, 0.2)), 0.05, 0.5)
    stor_power = jnp.clip(jnp.exp(math.log(2.0) - 1.89712 * jax.random.uniform(streams_of[11], (NSTOR,), jnp.float32) ** block_scale(streams_of[11], (NSTOR,), ((0, 4),), -0.2, 0.2)), 0.3, 2.0)
    stor_loss = jnp.clip(jnp.exp(math.log(0.3) - 2.7080503 * jax.random.uniform(streams_of[12], (NSTOR,), jnp.float32) ** block_scale(streams_of[12], (NSTOR,), ((0, 4),), -0.2, 0.2)), 0.02, 0.3)
    stor_cap = jnp.clip(0.5 + 2.5 * jax.random.uniform(streams_of[13], (NSTOR,), jnp.float32) ** block_scale(streams_of[13], (NSTOR,), ((0, 4),), -0.2, 0.2), 0.5, 3.0)
    flow_limit = jnp.clip(jnp.exp(jax.random.uniform(streams_of[14], (LINES,), jnp.float32, math.log(0.5), math.log(2.0))), 0.5, 2.0)
    return {"gen_start": gen_start, "charge_start": charge_start, "load": load, "ptdf_tiles": ptdf_tiles, "tile_row": tile_row, "tile_col": tile_col, "gen_bus": gen_bus, "stor_bus": stor_bus, "gen_cost": gen_cost, "gen_max": gen_max, "ramp_limit": ramp_limit, "stor_power": stor_power, "stor_loss": stor_loss, "stor_cap": stor_cap, "flow_limit": flow_limit}


TAU = 0.5
SIGMA = 0.5


def forward_state(inputs, log_keep):
    retention = jnp.exp(log_keep)

    def advance(carried, column):
        carried = retention * carried + column
        return carried, carried

    anchor = jnp.zeros(inputs.shape[1], jnp.float32)
    finish, running = lax.scan(advance, anchor, inputs)
    length = inputs.shape[0]
    closed = finish / (1.0 - jnp.exp(length * log_keep))
    steps_in = jnp.arange(1, length + 1, dtype=jnp.int32).astype(jnp.float32)[:, None]
    return running + jnp.exp(steps_in * log_keep[None, :]) * closed[None, :]


def backward_state(inputs, log_keep):
    retention = jnp.exp(log_keep)

    def advance(carried, column):
        carried = retention * carried + column
        return carried, carried

    anchor = jnp.zeros(inputs.shape[1], jnp.float32)
    finish, running = lax.scan(advance, anchor, inputs, reverse=True)
    length = inputs.shape[0]
    closed = finish / (1.0 - jnp.exp(length * log_keep))
    steps_in = (length - jnp.arange(length, dtype=jnp.int32)).astype(jnp.float32)[:, None]
    return running + jnp.exp(steps_in * log_keep[None, :]) * closed[None, :]


def reference(gen_start, charge_start, load, ptdf_tiles, tile_row, tile_col, gen_bus, stor_bus, gen_cost, gen_max, ramp_limit, stor_power, stor_loss, stor_cap, flow_limit):
    gen_global = (jnp.arange(NGEN, dtype=jnp.int32) // G_DEV) * BUS_DEV + gen_bus
    stor_global = (jnp.arange(NSTOR, dtype=jnp.int32) // S_DEV) * BUS_DEV + stor_bus
    tiles_blocks = ptdf_tiles.reshape(N_BUS, KT, TILE, TILE)
    rows_blocks = tile_row.reshape(N_BUS, KT)
    cols_blocks = tile_col.reshape(N_BUS, KT)
    log_keep = jnp.log1p(-stor_loss)
    generation = gen_start
    charging = charge_start
    line_dual = jnp.zeros((HOURS, LINES), jnp.float32)
    ramp_dual = jnp.zeros((HOURS, NGEN), jnp.float32)
    state_dual = jnp.zeros((HOURS, NSTOR), jnp.float32)
    balance_dual = jnp.zeros((HOURS,), jnp.float32)
    negative_load = -load.astype(jnp.float32)
    for iteration in range(ITERS):
        injection = negative_load.at[:, gen_global].add(generation)
        injection = injection.at[:, stor_global].add(-charging)
        injection_half = injection.astype(jnp.bfloat16)
        injection_blocks = jnp.transpose(injection_half.reshape(HOURS, N_BUS, BUS_DEV), (1, 0, 2))

        def block_flows(totals, pieces):
            injection_block, tiles_block, rows_block, cols_block = pieces
            picked = injection_block.reshape(HOURS, CTILES, TILE)[:, cols_block, :].astype(jnp.float32)
            products = jnp.einsum("hkc,kjc->hkj", picked, tiles_block.astype(jnp.float32), precision=lax.Precision.HIGHEST)
            partial_flows = jnp.zeros((HOURS, LTILES, TILE), jnp.float32).at[:, rows_block, :].add(products)
            partial_half = lax.optimization_barrier(partial_flows.reshape(HOURS, LINES).astype(jnp.bfloat16))
            return totals + partial_half.astype(jnp.float32), None

        line_flows, _ = lax.scan(block_flows, jnp.zeros((HOURS, LINES), jnp.float32), (injection_blocks, tiles_blocks, rows_blocks, cols_blocks))
        balance = jnp.sum(injection, axis=1)
        ramp_step = generation - jnp.roll(generation, 1, axis=0)
        charge_state = forward_state(charging, log_keep)
        line_shift = line_dual + SIGMA * line_flows
        line_next = line_shift - jnp.clip(line_shift, -SIGMA * flow_limit[None, :], SIGMA * flow_limit[None, :])
        ramp_shift = ramp_dual + SIGMA * ramp_step
        ramp_next = ramp_shift - jnp.clip(ramp_shift, -SIGMA * ramp_limit[None, :], SIGMA * ramp_limit[None, :])
        state_shift = state_dual + SIGMA * charge_state
        state_next = state_shift - jnp.clip(state_shift, 0.0, SIGMA * stor_cap[None, :])
        balance_next = balance_dual + (SIGMA / NGEN) * balance
        line_bar = 2.0 * line_next - line_dual
        ramp_bar = 2.0 * ramp_next - ramp_dual
        state_bar = 2.0 * state_next - state_dual
        balance_bar = 2.0 * balance_next - balance_dual
        line_dual, ramp_dual, state_dual, balance_dual = line_next, ramp_next, state_next, balance_next
        bar_half = line_bar.astype(jnp.bfloat16)

        def block_prices(pieces):
            tiles_block, rows_block, cols_block = pieces
            line_rows = bar_half.reshape(HOURS, LTILES, TILE)[:, rows_block, :].astype(jnp.float32)
            transposed = jnp.einsum("hkj,kjc->hkc", line_rows, tiles_block.astype(jnp.float32), precision=lax.Precision.HIGHEST)
            return jnp.zeros((HOURS, CTILES, TILE), jnp.float32).at[:, cols_block, :].add(transposed).reshape(HOURS, BUS_DEV)

        prices = lax.map(block_prices, (tiles_blocks, rows_blocks, cols_blocks))
        bus_price = jnp.transpose(prices, (1, 0, 2)).reshape(HOURS, NBUS)
        ramp_adjoint = ramp_bar - jnp.roll(ramp_bar, -1, axis=0)
        storage_term = backward_state(state_bar, log_keep)
        gen_slope = gen_cost[None, :] + balance_bar[:, None] + bus_price[:, gen_global] + ramp_adjoint
        generation = jnp.clip(generation - TAU * gen_slope, 0.0, gen_max[None, :])
        charge_slope = storage_term - balance_bar[:, None] - bus_price[:, stor_global]
        charging = jnp.clip(charging - TAU * charge_slope, -stor_power[None, :], stor_power[None, :])
    return generation, charging, line_dual
```

```python
import functools

import jax
import jax.numpy as jnp
from jax import lax
from jax.experimental import pallas as pl
from jax.experimental.pallas import tpu as pltpu
from jax.sharding import PartitionSpec as P

ITERS = 3
TAU = 0.5
SIGMA = 0.5
LANE = 128
GROUP = 8
F32 = jnp.float32
BF16 = jnp.bfloat16

NN = (((1,), (0,)), ((), ()))
NT = (((1,), (1,)), ((), ()))


def mxu(a, b, dims):
    return lax.dot_general(a, b, dims, preferred_element_type=F32)


def smem():
    return pl.BlockSpec(memory_space=pltpu.SMEM)


def vmem():
    return pl.BlockSpec(memory_space=pltpu.VMEM)


def hbm():
    return pl.BlockSpec(memory_space=pl.ANY)


def params():
    return pltpu.CompilerParams(vmem_limit_bytes=52 * 1024 * 1024)


def plan(tile_row, tile_col, unit_bus, mine, quarter_tiles, bus_tiles):
    kt, units = tile_row.shape[0], unit_bus.shape[0]
    ids = jnp.arange(units, dtype=jnp.int32)
    key = unit_bus * units + ids
    rank = jnp.sum((key[None, :] < key[:, None]).astype(jnp.int32), axis=1)
    place = rank[:, None] == ids[None, :]
    sorted_bus = jnp.sum(jnp.where(place, unit_bus[:, None], 0), axis=0)
    place = place.astype(BF16)
    edges = jnp.arange(bus_tiles + 1, dtype=jnp.int32) * LANE
    starts = jnp.sum((unit_bus[None, :] < edges[:, None]).astype(jnp.int32), axis=1)
    relative = ((tile_row // quarter_tiles) ^ mine) * quarter_tiles + tile_row % quarter_tiles
    tiles = jnp.arange(kt, dtype=jnp.int32)
    tile_key = relative * kt + tiles
    tile_rank = jnp.sum((tile_key[None, :] < tile_key[:, None]).astype(jnp.int32), axis=1)
    packed = (relative * bus_tiles + tile_col) * kt + tiles
    packed = jnp.sum(jnp.where(tile_rank[:, None] == tiles[None, :], packed[:, None], 0), axis=0)
    order = packed % kt
    packed = packed // kt
    return place, sorted_bus[None, :], starts, packed // bus_tiles, packed % bus_tiles, order


def build_kernel(
    cap, chunks, quarter_tiles,
    starts, rows, cols, order, sorted_bus, tiles, load,
    ent_row, ent_blk, ptr, compact, base, load_sum,
    ent_tile, ent_col, scratch, sems,
):
    kt = tiles.shape[0]
    hours = load.shape[0]
    dummy = chunks * quarter_tiles

    def pad(at):
        def put(i, at):
            @pl.when(at % GROUP != 0)
            def _():
                ent_row[at] = dummy
                ent_blk[at] = 0
                ent_tile[at] = 0
                ent_col[at] = 0

            return jnp.where(at % GROUP != 0, at + 1, at)

        return lax.fori_loop(0, GROUP - 1, put, at)

    def per_tile(k, carry):
        at, chunk = carry
        row, col = rows[k], cols[k]
        now = row // quarter_tiles

        def next_chunk(state):
            at, chunk = state
            at = pad(at)
            ptr[chunk + 1] = at // GROUP
            return at, chunk + 1

        at, chunk = lax.while_loop(lambda s: s[1] < now, next_chunk, (at, chunk))
        lo, hi = starts[col], starts[col + 1]
        first = lo // LANE
        last = jnp.where(hi > lo, (hi - 1) // LANE + 1, first)

        def put(m, at):
            ent_row[at] = row
            ent_blk[at] = m
            ent_tile[at] = order[k]
            ent_col[at] = col
            return at + 1

        return lax.fori_loop(first, last, put, at), chunk

    ptr[0] = 0
    at, chunk = lax.fori_loop(0, kt, per_tile, (jnp.int32(0), jnp.int32(0)))

    def close(state):
        at, chunk = state
        at = pad(at)
        ptr[chunk + 1] = at // GROUP
        return at, chunk + 1

    lax.while_loop(lambda s: s[1] < chunks, close, (at, chunk))
    groups = ptr[chunks]

    line = lax.broadcasted_iota(jnp.int32, (LANE, LANE), 0)

    def compress(n, _):
        for u in range(GROUP):
            e = n * GROUP + u
            hot = (line + ent_col[e] * LANE == sorted_bus[ent_blk[e]]).astype(F32).astype(BF16)
            scratch[e] = mxu(tiles[ent_tile[e]], hot, NN).astype(BF16)
        span = pl.ds(n * GROUP, GROUP)
        pltpu.make_async_copy(scratch.at[span], compact.at[span], sems.at[n]).start()
        return 0

    lax.fori_loop(0, groups, compress, 0)
    base[...] = jnp.zeros_like(base)
    unroll = 4 if kt % 4 == 0 else 1

    def loads(n, _):
        for u in range(unroll):
            k = n * unroll + u
            base[rows[k]] -= mxu(load[cols[k]], tiles[order[k]], NT)
        return 0

    lax.fori_loop(0, kt // unroll, loads, 0)
    total = load[0].astype(F32)
    for c in range(1, load.shape[0]):
        total += load[c].astype(F32)
    load_sum[...] = jnp.sum(total, axis=1, keepdims=True)

    def drain(n, _):
        span = pl.ds(n * GROUP, GROUP)
        pltpu.make_async_copy(scratch.at[span], compact.at[span], sems.at[n]).wait()
        return 0

    lax.fori_loop(0, groups, drain, 0)


def fetch(compact, held, sems, first, last):
    def start(n, _):
        span = pl.ds(n * GROUP, GROUP)
        pltpu.make_async_copy(compact.at[span], held.at[span], sems.at[n]).start()
        return 0

    lax.fori_loop(first, last, start, 0)


def arrived(compact, held, sems, n):
    span = pl.ds(n * GROUP, GROUP)
    pltpu.make_async_copy(compact.at[span], held.at[span], sems.at[n]).wait()


def flow_kernel(
    chunks, quarter_tiles,
    ent_row, ent_blk, ptr, generation, charging, place, base, load_sum, compact,
    *rest,
):
    outs = rest[:chunks]
    balance, held, picked, total, sems = rest[chunks:]
    groups = ptr[chunks]
    fetch(compact, held, sems, 0, groups)
    gens = generation.shape[1]
    g, p = generation[...], charging[...]
    balance[...] = (
        jnp.sum(g, axis=1, keepdims=True) - jnp.sum(p, axis=1, keepdims=True) - load_sum[...]
    )
    chosen = mxu(g.astype(BF16), place[:gens], NN) - mxu(p.astype(BF16), place[gens:], NN)
    chosen = chosen.astype(BF16)
    for m in range(picked.shape[0]):
        picked[m] = chosen[:, m * LANE : (m + 1) * LANE]
    total[: chunks * quarter_tiles] = base[...]

    def group(n, _):
        arrived(compact, held, sems, n)
        for u in range(GROUP):
            e = n * GROUP + u
            total[ent_row[e]] += mxu(picked[ent_blk[e]], held[e], NT)
        return 0

    lax.fori_loop(0, groups, group, 0)
    for d in range(chunks):
        for j in range(quarter_tiles):
            outs[d][:, j * LANE : (j + 1) * LANE] = total[d * quarter_tiles + j].astype(BF16)


def price_kernel(
    chunks, quarter_tiles,
    ent_row, ent_blk, ptr, *rest,
):
    bars = rest[:chunks]
    (place, compact, generation, charging, fixed_g, fixed_p, bb, gen_max, power,
     next_g, next_p, held, lines, total, sems) = rest[chunks:]
    groups = ptr[chunks]
    fetch(compact, held, sems, 0, groups)
    hours = generation.shape[0]
    gens = generation.shape[1]
    for d in range(chunks):
        for j in range(quarter_tiles):
            lines[d * quarter_tiles + j] = bars[d][:, j * LANE : (j + 1) * LANE]
    lines[chunks * quarter_tiles] = jnp.zeros((hours, LANE), BF16)
    total[...] = jnp.zeros_like(total)

    def group(n, _):
        arrived(compact, held, sems, n)
        for u in range(GROUP):
            e = n * GROUP + u
            total[ent_blk[e]] += mxu(lines[ent_row[e]], held[e], NN)
        return 0

    lax.fori_loop(0, groups, group, 0)
    price = jnp.concatenate([total[m] for m in range(total.shape[0])], axis=1)
    high = price.astype(BF16)
    low = (price - high.astype(F32)).astype(BF16)
    price = mxu(high, place[...], NT) + mxu(low, place[...], NT)
    g = generation[...] - TAU * (bb[...] + price[:, :gens] + fixed_g[...])
    next_g[...] = jnp.minimum(jnp.maximum(g, 0.0), gen_max[...])
    p = charging[...] - TAU * (fixed_p[...] - bb[...] - price[:, gens:])
    next_p[...] = jnp.minimum(jnp.maximum(p, -power[...]), power[...])


def hourly_kernel(
    years, hours, rows_each,
    where, everyone, generation, cost, ramp_limit, log_keep, cap,
    ramp_dual, state_dual,
    fixed_g, fixed_p, ramp_out, state_out, wide, local, bars,
):
    units = log_keep.shape[1]
    gens = generation.shape[1]
    me = where[0]
    before = lax.rem(me + years - 1, years)
    after = lax.rem(me + 1, years)
    wide[7:8] = everyone[before, hours + 1 : hours + 2, :gens]
    wide[8 : 8 + hours] = generation[...]
    wide[8 + hours : 9 + hours] = everyone[after, hours : hours + 1, :gens]
    ramps = wide[8 : 16 + hours] - wide[7 : 15 + hours]
    old = ramp_dual[...]
    shift = old + SIGMA * ramps
    limit = SIGMA * ramp_limit[...]
    new = shift - jnp.minimum(jnp.maximum(shift, -limit), limit)
    ramp_out[...] = new
    wide[0 : 8 + hours] = 2.0 * new - old
    fixed_g[...] = cost[...] + wide[0:hours] - wide[1 : 1 + hours]

    keep = log_keep[...]
    step = lax.broadcasted_iota(jnp.int32, (8, units), 0)
    rise = jnp.exp((step + 1).astype(F32) * keep)
    fall = jnp.exp((8 - step).astype(F32) * keep)
    one, two, four, eight = (jnp.exp(k * keep) for k in (1.0, 2.0, 4.0, 8.0))
    closing = 1.0 / (1.0 - jnp.exp(float(years * hours) * keep))
    count = years * hours // 8
    per = hours // 8

    def within(n, _):
        y = everyone[n // per, pl.ds((n % per) * 8, 8), :units]
        for by, factor in ((1, one), (2, two), (4, four)):
            y = y + jnp.where(step >= by, factor * pltpu.roll(y, by, 0), 0.0)
        local[n] = y
        return 0

    lax.fori_loop(0, count, within, 0, unroll=8)
    zero = jnp.zeros((1, units), F32)
    finish = lax.fori_loop(
        0, count, lambda n, c: local[n][7:8] + eight * c, zero, unroll=8
    )

    def forward(n, c):
        y = local[n]
        state = y + rise * c
        old = state_dual[n]
        shift = old + SIGMA * state
        new = shift - jnp.minimum(jnp.maximum(shift, 0.0), SIGMA * cap[...])
        state_out[n] = new
        bar = 2.0 * new - old
        for by, factor in ((1, one), (2, two), (4, four)):
            bar = bar + jnp.where(step < 8 - by, factor * pltpu.roll(bar, 8 - by, 0), 0.0)
        bars[n] = bar
        return y[7:8] + eight * c

    lax.fori_loop(0, count, forward, finish * closing, unroll=8)

    def back(i, c):
        return bars[count - 1 - i][0:1] + eight * c

    finish = lax.fori_loop(0, count, back, zero, unroll=8)
    start = lax.fori_loop(0, count - (me + 1) * per, back, finish * closing)

    c = start
    for j in reversed(range(per)):
        y = bars[me * per + j]
        fixed_p[8 * j : 8 * j + 8] = y + fall * c
        c = y[0:1] + eight * c


def shards(
    gen_start, charge_start, load, ptdf_tiles, tile_row, tile_col, gen_bus, stor_bus,
    gen_cost, gen_max, ramp_limit, stor_power, stor_loss, stor_cap, flow_limit,
):
    hours, gens = gen_start.shape
    stores = charge_start.shape[1]
    units = gens + stores
    kt = ptdf_tiles.shape[0]
    bus_tiles = load.shape[1] // LANE
    chunks = lax.axis_size("bus")
    years = lax.axis_size("tm")
    lines = flow_limit.shape[0] // chunks
    quarter_tiles = lines // LANE
    blocks = units // LANE
    line_tiles = chunks * quarter_tiles
    mine = lax.axis_index("bus")
    balance_step = SIGMA / (gens * chunks)
    cap = -(-(blocks * kt + chunks * GROUP) // 16) * 16

    place, sorted_bus, starts, rows, cols, order = plan(
        tile_row, tile_col, jnp.concatenate([gen_bus, stor_bus]), mine, quarter_tiles, bus_tiles
    )
    load_tiles = load.reshape(hours, bus_tiles, LANE).transpose(1, 0, 2)
    ent_row, ent_blk, ptr, compact, base, load_sum = pl.pallas_call(
        functools.partial(build_kernel, cap, chunks, quarter_tiles),
        out_shape=(
            jax.ShapeDtypeStruct((cap,), jnp.int32),
            jax.ShapeDtypeStruct((cap,), jnp.int32),
            jax.ShapeDtypeStruct((chunks + 1,), jnp.int32),
            jax.ShapeDtypeStruct((cap, LANE, LANE), BF16),
            jax.ShapeDtypeStruct((line_tiles, hours, LANE), F32),
            jax.ShapeDtypeStruct((hours, 1), F32),
        ),
        in_specs=[smem()] * 4 + [vmem()] * 3,
        out_specs=(smem(), smem(), smem(), hbm(), vmem(), vmem()),
        scratch_shapes=[
            pltpu.SMEM((cap,), jnp.int32),
            pltpu.SMEM((cap,), jnp.int32),
            pltpu.VMEM((cap, LANE, LANE), BF16),
            pltpu.SemaphoreType.DMA((cap // GROUP,)),
        ],
        compiler_params=params(),
        name="build",
    )(starts, rows, cols, order, sorted_bus.reshape(blocks, 1, LANE), ptdf_tiles, load_tiles)

    flows_call = pl.pallas_call(
        functools.partial(flow_kernel, chunks, quarter_tiles),
        out_shape=tuple(jax.ShapeDtypeStruct((hours, lines), BF16) for _ in range(chunks))
        + (jax.ShapeDtypeStruct((hours, 1), F32),),
        in_specs=[smem()] * 3 + [vmem()] * 5 + [hbm()],
        out_specs=tuple(vmem() for _ in range(chunks + 1)),
        scratch_shapes=[
            pltpu.VMEM((cap, LANE, LANE), BF16),
            pltpu.VMEM((blocks, hours, LANE), BF16),
            pltpu.VMEM((line_tiles + 1, hours, LANE), F32),
            pltpu.SemaphoreType.DMA((cap // GROUP,)),
        ],
        compiler_params=params(),
        name="flows",
    )
    price_call = pl.pallas_call(
        functools.partial(price_kernel, chunks, quarter_tiles),
        out_shape=(
            jax.ShapeDtypeStruct((hours, gens), F32),
            jax.ShapeDtypeStruct((hours, stores), F32),
        ),
        in_specs=[smem()] * 3 + [vmem()] * (chunks + 1) + [hbm()] + [vmem()] * 7,
        out_specs=(vmem(), vmem()),
        scratch_shapes=[
            pltpu.VMEM((cap, LANE, LANE), BF16),
            pltpu.VMEM((line_tiles + 1, hours, LANE), BF16),
            pltpu.VMEM((blocks, hours, LANE), F32),
            pltpu.SemaphoreType.DMA((cap // GROUP,)),
        ],
        compiler_params=params(),
        name="prices",
    )
    width = max(gens, stores)
    rows_each = hours + 8
    groups = years * hours // 8
    hourly_call = pl.pallas_call(
        functools.partial(hourly_kernel, years, hours, rows_each),
        out_shape=(
            jax.ShapeDtypeStruct((hours, gens), F32),
            jax.ShapeDtypeStruct((hours, stores), F32),
            jax.ShapeDtypeStruct((hours + 8, gens), F32),
            jax.ShapeDtypeStruct((groups, 8, stores), F32),
        ),
        in_specs=[smem()] + [vmem()] * 8,
        out_specs=(vmem(),) * 4,
        scratch_shapes=[
            pltpu.VMEM((hours + 16, gens), F32),
            pltpu.VMEM((groups, 8, stores), F32),
            pltpu.VMEM((groups, 8, stores), F32),
        ],
        compiler_params=params(),
        name="hourly",
    )

    where = lax.axis_index("tm").astype(jnp.int32).reshape(1)
    log_keep = jnp.log1p(-stor_loss)[None, :]
    limits = lax.dynamic_slice_in_dim(flow_limit, mine * lines, lines)[None, :] * SIGMA
    gen_max, power = gen_max[None, :], stor_power[None, :]
    cost, ramp_limit, stor_cap = gen_cost[None, :], ramp_limit[None, :], stor_cap[None, :]

    def swap(x, bit):
        return lax.ppermute(x, "bus", [(i, i ^ bit) for i in range(chunks)])

    bits = [1 << b for b in range(chunks.bit_length() - 1)]
    line_dual = jnp.zeros((hours, lines), F32)
    ramp_dual = jnp.zeros((hours + 8, gens), F32)
    state_dual = jnp.zeros((groups, 8, stores), F32)
    balance_dual = jnp.zeros((hours, 1), F32)
    g, p = gen_start, charge_start
    for _ in range(ITERS):
        sent = jnp.concatenate(
            [
                jnp.pad(p, ((0, 0), (0, width - stores))),
                jnp.pad(g[:1], ((0, 0), (0, width - gens))),
                jnp.pad(g[-1:], ((0, 7 - 1), (0, width - gens))),
            ]
        )
        everyone = lax.all_gather(sent, "tm")
        *parts, balance = flows_call(
            ent_row, ent_blk, ptr, g, p, place, base, load_sum, compact
        )
        parts = [[part] for part in parts]
        for at, bit in enumerate(bits):
            for d in reversed(range(chunks)):
                if d & bit and not d & (bit - 1):
                    got = swap(
                        sum(x.astype(F32) for x in parts[d]).astype(BF16), bit
                    )
                    parts[d ^ bit].append(got)
            balance = balance + swap(balance, bit)
        flows = sum(x.astype(F32) for x in parts[0])
        shift = line_dual + SIGMA * flows
        line_next = shift - jnp.clip(shift, -limits, limits)
        bar = (2.0 * line_next - line_dual).astype(BF16)
        line_dual = line_next
        have = {0: bar}
        for bit in reversed(bits):
            for d in list(have):
                have[d | bit] = swap(have[d], bit)
        balance_next = balance_dual + balance_step * balance
        bb = 2.0 * balance_next - balance_dual
        balance_dual = balance_next
        fixed_g, fixed_p, ramp_dual, state_dual = hourly_call(
            where, everyone, g, cost, ramp_limit, log_keep, stor_cap, ramp_dual, state_dual
        )
        g, p = price_call(
            ent_row, ent_blk, ptr, *[have[d] for d in range(chunks)],
            place, compact, g, p, fixed_g, fixed_p, bb, gen_max, power,
        )
    return g, p, line_dual


def solution(mesh):
    rows = P(("scen", "tm"), "bus")
    return jax.shard_map(
        shards,
        mesh=mesh,
        in_specs=(rows, rows, rows, P("bus", None, None)) + (P("bus"),) * 10 + (P(),),
        out_specs=(rows, rows, rows),
        check_vma=False,
    )
```

```python
import functools

import jax
import jax.numpy as jnp
from jax import lax
from jax.experimental import pallas as pl
from jax.experimental.pallas import tpu as pltpu
from jax.sharding import PartitionSpec as P

ITERS = 3
TAU = 0.5
SIGMA = 0.5
LANE = 128
LARGE, SMALL = 32, 8
KEPT = 160
F32 = jnp.float32
BF16 = jnp.bfloat16

NN = (((1,), (0,)), ((), ()))
NT = (((1,), (1,)), ((), ()))


def mxu(a, b, dims):
    return lax.dot_general(a, b, dims, preferred_element_type=F32)


def smem():
    return pl.BlockSpec(memory_space=pltpu.SMEM)


def vmem():
    return pl.BlockSpec(memory_space=pltpu.VMEM)


def hbm():
    return pl.BlockSpec(memory_space=pl.ANY)


def params(mib):
    return pltpu.CompilerParams(vmem_limit_bytes=mib * 1024 * 1024)


def cost(us):
    return pl.CostEstimate(flops=0, bytes_accessed=int(us * 3.0e6), transcendentals=0)


def lanes(at):
    return pl.ds(pl.multiple_of(at * LANE, LANE), LANE)


ROW, BLOCK, TILE, COLUMN, FIRST, START = range(6)


def plan_kernel(
    chunks, quarter_tiles,
    mine, gen_bus, stor_bus, tile_row, tile_col,
    place, sorted_bus, ents,
    tiles,
):
    units = place.shape[0]
    blocks = units // LANE
    kt = tile_row.shape[1]
    square = (LANE, LANE)
    sub = lax.broadcasted_iota(jnp.int32, square, 0).astype(F32)
    lane = lax.broadcasted_iota(jnp.int32, square, 1).astype(F32)
    eye = sub == lane

    def column(row):
        return jnp.sum(jnp.where(eye, jnp.broadcast_to(row, square), 0.0), axis=1, keepdims=True)

    def over_sub(mask, values):
        return jnp.sum(jnp.where(mask, values, 0.0), axis=0, keepdims=True)

    def over_lane(mask, values):
        return jnp.sum(jnp.where(mask, values, 0.0), axis=1, keepdims=True)

    bus = jnp.concatenate([gen_bus[...], stor_bus[...]], axis=1).astype(F32)
    unit = lax.broadcasted_iota(jnp.int32, (1, units), 1).astype(F32)
    key = bus * units + unit
    ordered = jnp.zeros((1, units), F32)
    starts = jnp.zeros((1, LANE), F32)
    stops = jnp.zeros((1, LANE), F32)
    for b in range(blocks):
        here = column(bus[:, b * LANE : (b + 1) * LANE])
        rank = over_lane(key < here * units + (sub[:, :1] + float(b * LANE)), 1.0)
        mine_at = rank == unit
        place[b * LANE : (b + 1) * LANE] = jnp.where(mine_at, 1.0, 0.0).astype(BF16)
        ordered += over_sub(mine_at, here)
        starts += over_sub(here < lane * LANE, 1.0)
        stops += over_sub(here < (lane + 1.0) * LANE, 1.0)
    for b in range(blocks):
        sorted_bus[b] = jnp.broadcast_to(column(ordered[:, b * LANE : (b + 1) * LANE]), square)

    tiles[...] = jnp.zeros_like(tiles)
    tiles[0:1, :kt] = tile_row[...]
    tiles[1:2, :kt] = tile_col[...]
    row, col = tiles[0:1], tiles[1:2].astype(F32)
    chunk = jnp.zeros_like(row)
    for d in range(1, chunks):
        chunk = chunk + (row >= d * quarter_tiles).astype(jnp.int32)
    relative = (((chunk ^ mine[0]) - chunk) * quarter_tiles + row).astype(F32)
    number = lane[:1]
    tile_key = jnp.where(number < kt, relative, float(chunks * quarter_tiles)) * LANE + number
    rank = over_sub(column(tile_key) < tile_key, 1.0)
    sorting = rank == sub
    relative, col, tile = (over_lane(sorting, x) for x in (relative, col, number))
    first, last = over_lane(lane == col, starts), over_lane(lane == col, stops)
    block = jnp.minimum(jnp.floor(first * (1.0 / LANE)), float(blocks - 1))
    until = jnp.floor((last - 1.0) * (1.0 / LANE))
    count = jnp.where(last > first, until - block + 1.0, 1.0)
    count = jnp.where(sub[:, :1] < kt, count, 0.0)
    at = over_lane(lane < sub, over_sub(eye, count))
    entry = lax.broadcasted_iota(jnp.int32, (1, ents.shape[1]), 1).astype(F32)
    inside = (at <= entry) & (entry < at + count)
    ents[...] = jnp.zeros_like(ents)
    for name, values in (
        (ROW, relative),
        (BLOCK, block - at + entry),
        (TILE, tile),
        (COLUMN, col),
        (FIRST, (entry == at).astype(F32)),
    ):
        ents[name : name + 1] = over_sub(inside, values).astype(jnp.int32)
    ents[START : START + 1, :LANE] = over_sub(relative < lane * quarter_tiles, count).astype(
        jnp.int32
    )


def sweep(lo, hi, body):
    hi = jnp.maximum(lo, hi)
    long = (hi - lo) // LARGE

    def group(n, _):
        for u in range(LARGE):
            body(lo + n * LARGE + u, None)
        return 0

    lax.fori_loop(0, long, group, 0)
    rest = lo + long * LARGE

    def short(n, _):
        for u in range(SMALL):
            e = rest + n * SMALL + u
            body(e, e < hi)
        return 0

    lax.fori_loop(0, (hi - rest + SMALL - 1) // SMALL, short, 0)


def sweep_held(lo, hi, compact, spill, stage, sem, body):
    kept = compact.shape[0] - SMALL
    sweep(lo, jnp.minimum(hi, kept), lambda e, live: body(e, live, compact.at[e]))

    def fetched(e, _):
        copy = pltpu.make_async_copy(spill.at[e - kept], stage, sem)
        copy.start()
        copy.wait()
        body(e, None, stage)
        return 0

    lax.fori_loop(jnp.maximum(lo, kept), hi, fetched, 0)


def pick(live, value, other):
    return value if live is None else jnp.where(live, value, other)


def build(ents, sorted_bus, load, tiles, compact, spill, base, load_sum, stage, sem, found):
    kept = compact.shape[0] - SMALL
    hours = load.shape[0]
    spare = base.shape[1] // LANE - 1
    base[...] = jnp.zeros_like(base)
    lane = lax.broadcasted_iota(jnp.int32, (LANE, LANE), 1)

    def restricted(e, live):
        col = pick(live, ents[COLUMN, e], 0)
        row = jnp.where(pick(live, ents[FIRST, e], 0) == 1, ents[ROW, e], spare)
        bus = sorted_bus[pick(live, ents[BLOCK, e], 0)]
        hot = jnp.where(bus == (lane + col * LANE).astype(F32), 1.0, 0.0).astype(BF16)
        left = jnp.concatenate([load[:, lanes(col)], hot], axis=0)
        both = mxu(left, tiles[pick(live, ents[TILE, e], 0)], NT)
        base[:, lanes(row)] -= both[:hours]
        return both[hours:].astype(BF16)

    def keep(e, live):
        compact[e] = restricted(e, live)

    def put_out(e, _):
        stage[...] = restricted(e, None)
        copy = pltpu.make_async_copy(stage, spill.at[e - kept], sem)
        copy.start()
        copy.wait()
        return 0

    sweep(jnp.int32(0), jnp.minimum(found, kept), keep)
    lax.fori_loop(jnp.int32(kept), found, put_out, 0)
    total = load[:, :LANE].astype(F32)
    for c in range(1, load.shape[1] // LANE):
        total += load[:, c * LANE : (c + 1) * LANE].astype(F32)
    load_sum[...] = jnp.sum(total, axis=1, keepdims=True)


def add_flows(ents, compact, spill, stage, sem, picked, base, total, cap, chunks, quarter_tiles, first, last, outs):
    origin, width = first * quarter_tiles, (last - first) * quarter_tiles
    total[:, : width * LANE] = base[:, origin * LANE : (origin + width) * LANE]
    spare, blocks = width, picked.shape[0] - 1

    def entry(e, live, matrix):
        row = pick(live, ents[ROW, e] - origin, spare)
        m = pick(live, ents[BLOCK, e], blocks)
        total[:, lanes(row)] += mxu(picked[m], matrix[...], NN)

    lo, hi = ents[START, first], ents[START, last]
    sweep_held(lo, hi, compact, spill, stage, sem, entry)
    for d in range(last - first):
        at = d * quarter_tiles
        outs[d][...] = total[:, at * LANE : (at + quarter_tiles) * LANE].astype(BF16)


def add_prices(
    ents, compact, spill, stage, sem, bars, lines, total, cap, quarter_tiles, first, last
):
    half = (quarter_tiles + 1) // 2
    origin = first * quarter_tiles
    for d in range(last - first):
        at = d * quarter_tiles
        lines[:, at * LANE : (at + half) * LANE] = bars[2 * d][:, : half * LANE]
        lines[:, (at + half) * LANE : (at + quarter_tiles) * LANE] = bars[2 * d + 1][...]
    spare, blocks = (last - first) * quarter_tiles, total.shape[0] - 2

    def entry(e, live, matrix):
        row = pick(live, ents[ROW, e] - origin, spare)
        m = pick(live, ents[BLOCK, e], blocks)
        total[m] += mxu(lines[:, lanes(row)], matrix[...], NT)

    lo, hi = ents[START, first], ents[START, last]
    sweep_held(lo, hi, compact, spill, stage, sem, entry)
    for d in range(last - first):
        total[blocks + 1] += bars[2 * d][:, half * LANE :].astype(F32)


def choose(g, p, place, picked):
    x = jnp.concatenate([g.astype(BF16), (-p).astype(BF16)], axis=1)
    chosen = mxu(x, place[...], NN).astype(BF16)
    for m in range(picked.shape[0] - 1):
        picked[m] = chosen[:, m * LANE : (m + 1) * LANE]


def send_hours(g, p, sent):
    hours, stores = p.shape
    gens = g.shape[1]
    sent[:hours] = p
    sent[hours:] = jnp.zeros_like(sent[hours:])
    each = -(-gens // stores)
    for i, row in enumerate((g[:1], g[hours - 1 :])):
        for j in range(each):
            piece = row[:, j * stores : min((j + 1) * stores, gens)]
            sent[hours + i * each + j : hours + i * each + j + 1, : piece.shape[1]] = piece


def own_balance(g, p, load_sum, balance):
    value = jnp.sum(g, axis=1, keepdims=True) - jnp.sum(p, axis=1, keepdims=True) - load_sum[...]
    lane = lax.broadcasted_iota(jnp.int32, balance.shape, 1)
    high = value.astype(BF16).astype(F32)
    middle = (value - high).astype(BF16).astype(F32)
    low = value - high - middle
    balance[...] = jnp.where(
        lane == 0, high, jnp.where(lane == 1, middle, jnp.where(lane == 2, low, 0.0))
    ).astype(BF16)


def first_kernel(
    cap, chunks, quarter_tiles,
    ents, sorted_bus, load, tiles, place, generation, charging,
    compact, spill, base, load_sum, *rest,
):
    upper = chunks - chunks // 2
    outs = rest[:upper]
    balance, sent, picked, stage, sem, total = rest[upper:]
    g, p = generation[...], charging[...]
    send_hours(g, p, sent)
    choose(g, p, place, picked)
    found = ents[START, chunks]
    build(ents, sorted_bus, load, tiles, compact, spill, base, load_sum, stage, sem, found)
    own_balance(g, p, load_sum, balance)
    add_flows(
        ents, compact, spill, stage, sem, picked, base, total,
        cap, chunks, quarter_tiles, chunks // 2, chunks, outs,
    )


def lower_kernel(
    cap, chunks, quarter_tiles, first, last,
    ents, compact, spill, base, picked,
    *rest,
):
    outs = rest[: last - first]
    stage, sem, total = rest[last - first :]
    add_flows(
        ents, compact, spill, stage, sem, picked, base, total,
        cap, chunks, quarter_tiles, first, last, outs,
    )


def price_kernel(cap, quarter_tiles, first, last, fresh, ents, compact, spill, *rest):
    count = 2 * (last - first)
    bars, rest = rest[:count], rest[count:]
    if fresh:
        total, stage, sem, lines = rest
        total[...] = jnp.zeros_like(total)
    else:
        before, total, stage, sem, lines = rest
        total[...] = before[...]
    add_prices(
        ents, compact, spill, stage, sem, bars, lines, total, cap, quarter_tiles, first, last
    )


def step_kernel(
    cap, chunks, quarter_tiles, balance_step, final,
    ents, compact, spill, place, before, generation, charging, fixed_g, fixed_p, balance_dual,
    limits, base, load_sum, *rest,
):
    start = chunks - chunks // 4
    count = 2 * (chunks - start)
    bars, rest = rest[:count], rest[count:]
    if final:
        next_g, next_p, stage, sem, lines, prices = rest
    else:
        next_g, next_p, next_balance, *rest = rest
        outs, rest = rest[: chunks - chunks // 2], rest[chunks - chunks // 2 :]
        balance, sent, picked, stage, sem, lines, prices, total = rest
    prices[...] = before[...]
    add_prices(
        ents, compact, spill, stage, sem, bars, lines, prices, cap, quarter_tiles, start, chunks
    )
    hours, gens = generation.shape
    blocks = prices.shape[0] - 2
    price = jnp.concatenate([prices[m] for m in range(blocks)], axis=1)
    high = price.astype(BF16)
    low = (price - high.astype(F32)).astype(BF16)
    price = mxu(jnp.concatenate([high, low], axis=0), place[...], NT)
    price = price[:hours] + price[hours:]
    old = balance_dual[...]
    new = old + balance_step * jnp.sum(prices[blocks + 1], axis=1, keepdims=True)
    bb = 2.0 * new - old
    g = generation[...] - TAU * (bb + price[:, :gens] + fixed_g[...])
    bound = limits[1:2]
    g = jnp.minimum(jnp.maximum(g, 0.0), bound[:, :gens])
    p = charging[...] - TAU * (fixed_p[...] - bb - price[:, gens:])
    p = jnp.minimum(jnp.maximum(p, -bound[:, gens:]), bound[:, gens:])
    next_g[...] = g
    next_p[...] = p
    if not final:
        next_balance[...] = new
        send_hours(g, p, sent)
        own_balance(g, p, load_sum, balance)
        choose(g, p, place, picked)
        add_flows(
            ents, compact, spill, stage, sem, picked, base, total,
            cap, chunks, quarter_tiles, chunks // 2, chunks, outs,
        )


def hourly_kernel(
    years, hours, order,
    where, generation, limits, ramp_dual, state_dual,
    *rest,
):
    heard, rest = rest[:years], rest[years:]
    fixed_g, fixed_p, ramp_out, state_out, everyone, wide, local, bars = rest
    gens = generation.shape[1]
    units = limits.shape[1] - gens
    cost, ramp_limit = limits[0:1, :gens], limits[2:3, :gens]
    cap, keep = limits[2:3, gens:], limits[3:4, gens:]
    each = -(-gens // units)
    me = where[0]
    before = lax.rem(me + years - 1, years)
    after = lax.rem(me + 1, years)
    for j in range(years):
        everyone[me ^ order[j]] = heard[j][...]
    wide[8 : 8 + hours] = generation[...]
    for j in range(each):
        span = min(units, gens - j * units)
        to = slice(j * units, j * units + span)
        at = hours + each + j
        wide[7:8, to] = everyone[before, at : at + 1, :span]
        at = hours + j
        wide[8 + hours : 9 + hours, to] = everyone[after, at : at + 1, :span]
    ramps = wide[8 : 16 + hours] - wide[7 : 15 + hours]
    old = ramp_dual[...]
    shift = old + SIGMA * ramps
    limit = SIGMA * ramp_limit
    new = shift - jnp.minimum(jnp.maximum(shift, -limit), limit)
    ramp_out[...] = new
    wide[0 : 8 + hours] = 2.0 * new - old
    fixed_g[...] = cost + wide[0:hours] - wide[1 : 1 + hours]

    step = lax.broadcasted_iota(jnp.int32, (8, units), 0)
    rise = jnp.exp((step + 1).astype(F32) * keep)
    fall = jnp.exp((8 - step).astype(F32) * keep)
    one, two, four, eight = (jnp.exp(k * keep) for k in (1.0, 2.0, 4.0, 8.0))
    closing = 1.0 / (1.0 - jnp.exp(float(years * hours) * keep))
    count = years * hours // 8
    per = hours // 8

    def within(n, _):
        y = everyone[n // per, pl.ds(pl.multiple_of((n % per) * 8, 8), 8), :]
        for by, factor in ((1, one), (2, two), (4, four)):
            y = y + jnp.where(step >= by, factor * pltpu.roll(y, by, 0), 0.0)
        local[n] = y
        return 0

    lax.fori_loop(0, count, within, 0, unroll=8)
    zero = jnp.zeros((1, units), F32)
    finish = lax.fori_loop(0, count, lambda n, c: local[n][7:8] + eight * c, zero, unroll=8)

    def forward(n, c):
        y = local[n]
        state = y + rise * c
        old = state_dual[n]
        shift = old + SIGMA * state
        new = shift - jnp.minimum(jnp.maximum(shift, 0.0), SIGMA * cap)
        state_out[n] = new
        bar = 2.0 * new - old
        for by, factor in ((1, one), (2, two), (4, four)):
            bar = bar + jnp.where(step < 8 - by, factor * pltpu.roll(bar, 8 - by, 0), 0.0)
        bars[n] = bar
        return y[7:8] + eight * c

    lax.fori_loop(0, count, forward, finish * closing, unroll=8)

    def back(i, c):
        return bars[count - 1 - i][0:1] + eight * c

    finish = lax.fori_loop(0, count, back, zero, unroll=8)
    c = lax.fori_loop(0, count - (me + 1) * per, back, finish * closing)
    for j in reversed(range(per)):
        y = bars[me * per + j]
        fixed_p[8 * j : 8 * j + 8] = y + fall * c
        c = y[0:1] + eight * c


def shards(
    gen_start, charge_start, load, ptdf_tiles, tile_row, tile_col, gen_bus, stor_bus,
    gen_cost, gen_max, ramp_limit, stor_power, stor_loss, stor_cap, flow_limit,
):
    hours, gens = gen_start.shape
    stores = charge_start.shape[1]
    units = gens + stores
    kt = ptdf_tiles.shape[0]
    bus_tiles = load.shape[1] // LANE
    chunks = lax.axis_size("bus")
    years = lax.axis_size("tm")
    lines = flow_limit.shape[0] // chunks
    quarter_tiles = lines // LANE
    half = (quarter_tiles + 1) // 2 * LANE
    widths = (half, lines - half)
    blocks = units // LANE
    line_tiles = chunks * quarter_tiles
    mine = lax.axis_index("bus")
    balance_step = SIGMA / (gens * chunks)
    cap = blocks * kt + LARGE
    kept = min(cap, KEPT) // SMALL * SMALL
    sent_rows = -(-(hours + 2 * -(-gens // stores)) // 8) * 8
    groups = years * hours // 8

    def like(*shape, dtype=F32):
        return jax.ShapeDtypeStruct(shape, dtype)

    width = -(-(cap + SMALL) // LANE) * LANE
    place, sorted_bus, ents = pl.pallas_call(
        functools.partial(plan_kernel, chunks, quarter_tiles),
        out_shape=(
            like(units, units, dtype=BF16),
            like(blocks, LANE, LANE),
            like(8, width, dtype=jnp.int32),
        ),
        in_specs=[smem()] + [vmem()] * 4,
        out_specs=(vmem(),) * 3,
        scratch_shapes=[pltpu.VMEM((8, LANE), jnp.int32)],
        compiler_params=params(STEP_MIB),
        name="plan",
        cost_estimate=cost(3),
    )(
        mine.astype(jnp.int32).reshape(1),
        *[x[None, :] for x in (gen_bus, stor_bus, tile_row, tile_col)],
    )

    chunk_out = (like(hours, lines, dtype=BF16),) * (chunks // 2)
    staging = [pltpu.VMEM((LANE, LANE), BF16), pltpu.SemaphoreType.DMA]
    picked_shape = like(blocks + 1, hours, LANE, dtype=BF16)

    def flow_scratch(count):
        return [pltpu.VMEM((hours, (count * quarter_tiles + 1) * LANE), F32)]

    def line_scratch(count):
        return pltpu.VMEM((hours, (count * quarter_tiles + 1) * LANE), BF16)

    price_shape = (blocks + 2, hours, LANE)
    first_call = pl.pallas_call(
        functools.partial(first_kernel, cap, chunks, quarter_tiles),
        out_shape=(
            like(kept + SMALL, LANE, LANE, dtype=BF16),
            like(max(cap - kept, SPILL), LANE, LANE, dtype=BF16),
            like(hours, (line_tiles + 1) * LANE),
            like(hours, 1),
        )
        + chunk_out
        + (like(hours, LANE, dtype=BF16), like(sent_rows, stores), picked_shape),
        in_specs=[smem()] + [vmem()] * 6,
        out_specs=(vmem(), hbm()) + (vmem(),) * (chunks // 2 + 5),
        scratch_shapes=staging + flow_scratch(chunks // 2),
        compiler_params=params(STEP_MIB),
        name="first",
        cost_estimate=cost(9),
    )

    def lower_call(first, last):
        return pl.pallas_call(
            functools.partial(lower_kernel, cap, chunks, quarter_tiles, first, last),
            out_shape=(like(hours, lines, dtype=BF16),) * (last - first),
            in_specs=[smem(), vmem(), hbm()] + [vmem()] * 2,
            out_specs=(vmem(),) * (last - first),
            scratch_shapes=staging + flow_scratch(last - first),
            compiler_params=params(STEP_MIB),
            name="lower",
            cost_estimate=cost(2),
        )

    def price_call(first, last, fresh):
        return pl.pallas_call(
            functools.partial(price_kernel, cap, quarter_tiles, first, last, fresh),
            out_shape=like(*price_shape),
            in_specs=[smem(), vmem(), hbm()] + [vmem()] * (2 * (last - first) + (not fresh)),
            out_specs=vmem(),
            scratch_shapes=staging + [line_scratch(last - first)],
            compiler_params=params(STEP_MIB),
            name="price",
            cost_estimate=cost(2),
        )

    tail = chunks - chunks // 4

    def step_call(final):
        shape = (like(hours, gens), like(hours, stores))
        scratch = staging + [line_scratch(chunks - tail), pltpu.VMEM(price_shape, F32)]
        if not final:
            shape += (like(hours, 1),) + chunk_out
            shape += (like(hours, LANE, dtype=BF16), like(sent_rows, stores), picked_shape)
            scratch += flow_scratch(chunks // 2)
        return pl.pallas_call(
            functools.partial(step_kernel, cap, chunks, quarter_tiles, balance_step, final),
            out_shape=shape,
            in_specs=[smem(), vmem(), hbm()] + [vmem()] * (10 + 2 * (chunks - tail)),
            out_specs=(vmem(),) * len(shape),
            scratch_shapes=scratch,
            compiler_params=params(STEP_MIB),
            name="step",
            cost_estimate=cost(4),
        )

    spans = [1 << b for b in reversed(range(years.bit_length() - 1))]
    order = [0]
    for bit in spans:
        order += [j ^ bit for j in order]

    hourly_call = pl.pallas_call(
        functools.partial(hourly_kernel, years, hours, order),
        out_shape=(
            like(hours, gens),
            like(hours, stores),
            like(hours + 8, gens),
            like(groups, 8, stores),
        ),
        in_specs=[smem()] + [vmem()] * (4 + years),
        out_specs=(vmem(),) * 4,
        scratch_shapes=[
            pltpu.VMEM((years, sent_rows, stores), F32),
            pltpu.VMEM((hours + 16, gens), F32),
            pltpu.VMEM((groups, 8, stores), F32),
            pltpu.VMEM((groups, 8, stores), F32),
        ],
        compiler_params=params(STEP_MIB),
        name="hourly",
            cost_estimate=cost(2.4),
    )

    where = lax.axis_index("tm").astype(jnp.int32).reshape(1)
    limits = lax.dynamic_slice_in_dim(flow_limit, mine * lines, lines)[None, :] * SIGMA
    limits = (limits[:, :half], limits[:, half:])
    unit_rows = jnp.stack(
        [
            jnp.concatenate([gen_cost, stor_power]),
            jnp.concatenate([gen_max, stor_power]),
            jnp.concatenate([ramp_limit, stor_cap]),
            jnp.concatenate([ramp_limit, jnp.log1p(-stor_loss)]),
        ]
    )

    def swap(x, bit, axis="bus"):
        size = lax.axis_size(axis)
        return lax.ppermute(x, axis, [(i, i ^ bit) for i in range(size)])

    def hear(stacked, over):
        for bit in over:
            stacked = jnp.concatenate([stacked, swap(stacked, bit, "tm")])
        return stacked

    def cut(xs, h):
        return [x[:, :half] if h == 0 else x[:, half:] for x in xs]

    bits = [1 << b for b in range(chunks.bit_length() - 1)]
    line_dual = [jnp.zeros((hours, w), F32) for w in widths]
    ramp_dual = jnp.zeros((hours + 8, gens), F32)
    state_dual = jnp.zeros((groups, 8, stores), F32)
    balance_dual = jnp.zeros((hours, 1), F32)
    g, p = gen_start, charge_start
    compact, spill, base, load_sum, *upper, balance, sent, picked = first_call(
        ents, sorted_bus, load, ptdf_tiles, place, g, p
    )
    half_way = chunks // 2

    def reduce(parts):
        for bit in bits[:-1]:
            for d in sorted(parts, reverse=True):
                if d & bit and not d & (bit - 1):
                    got = swap(sum(x.astype(F32) for x in parts[d]).astype(BF16), bit)
                    parts[d ^ bit].append(got)

    for iteration in range(ITERS):
        parts = {d: [x] for d, x in zip(range(half_way, chunks), upper)}
        reduce(parts)
        ready = [sum(x.astype(F32) for x in cut(parts[half_way], h)).astype(BF16) for h in (0, 1)]
        across = [swap(x, half_way) for x in ready]
        parts = {d: [] for d in range(half_way)}
        if half_way > 1:
            made = lower_call(1, half_way)(ents, compact, spill, base, picked)
            for d, x in zip(range(1, half_way), made):
                parts[d].append(x)
        sent, picked, *_ = lax.optimization_barrier((sent, picked, *ready))
        parts[0].append(lower_call(0, 1)(ents, compact, spill, base, picked)[0])
        reduce(parts)
        sent, parts[0][0] = lax.optimization_barrier((sent, parts[0][0]))
        heard = hear(sent[None], spans[:1])
        have = {0: []}
        for h in range(2):
            flows = sum(x.astype(F32) for x in cut(parts[0], h) + [across[h]])
            shift = line_dual[h] + SIGMA * flows
            after = shift - jnp.clip(shift, -limits[h], limits[h])
            bar = (2.0 * after - line_dual[h]).astype(BF16)
            line_dual[h] = after
            have[0].append(jnp.concatenate([bar, balance], axis=1) if h == 0 else bar)
            if h == 0:
                line_dual[1], have[0][0] = lax.optimization_barrier((line_dual[1], have[0][0]))
        have[half_way] = [swap(x, half_way) for x in have[0]]
        near = [0]
        for bit in reversed(bits[:-1]):
            for d in list(near):
                have[d | bit] = [swap(x, bit) for x in have[d]]
                near.append(d | bit)
        heard, *_ = lax.optimization_barrier((heard, have[near[-1]][1]))
        heard = hear(heard, spans[1:])
        prices = price_call(0, half_way, True)(
            ents, compact, spill, *[x for d in range(half_way) for x in have[d]]
        )
        heard, prices = lax.optimization_barrier((heard, prices))
        fixed_g, fixed_p, ramp_dual, state_dual = hourly_call(
            where, g, unit_rows, ramp_dual, state_dual, *[heard[j] for j in range(years)]
        )
        have[half_way][0], prices, fixed_g, fixed_p = lax.optimization_barrier(
            (have[half_way][0], prices, fixed_g, fixed_p)
        )
        far = [half_way]
        for bit in reversed(bits[:-1]):
            for d in list(far):
                have[d | bit] = [swap(x, bit) for x in have[d]]
                far.append(d | bit)
        if tail > half_way:
            prices = price_call(half_way, tail, False)(
                ents, compact, spill, *[x for d in range(half_way, tail) for x in have[d]], prices
            )
        final = iteration == ITERS - 1
        g, p, *rest = step_call(final)(
            ents, compact, spill, place, prices, g, p, fixed_g, fixed_p, balance_dual,
            unit_rows, base, load_sum, *[x for d in range(tail, chunks) for x in have[d]],
        )
        if not final:
            balance_dual, *upper, balance, sent, picked = rest
    return g, p, jnp.concatenate(line_dual, axis=1)


STEP_MIB = 16
SPILL = 1500


def solution(mesh):
    rows = P(("scen", "tm"), "bus")
    return jax.shard_map(
        shards,
        mesh=mesh,
        in_specs=(rows, rows, rows, P("bus", None, None)) + (P("bus"),) * 10 + (P(),),
        out_specs=(rows, rows, rows),
        check_vma=False,
    )
```

```python
import functools

import jax
import jax.numpy as jnp
from jax import lax
from jax.experimental import pallas as pl
from jax.experimental.pallas import tpu as pltpu
from jax.sharding import PartitionSpec as P

ITERS = 3
TAU = 0.5
SIGMA = 0.5
LANE = 128
LARGE, SMALL = 32, 8
KEPT = 160
F32 = jnp.float32
BF16 = jnp.bfloat16

NN = (((1,), (0,)), ((), ()))
NT = (((1,), (1,)), ((), ()))


def mxu(a, b, dims):
    return lax.dot_general(a, b, dims, preferred_element_type=F32)


def smem():
    return pl.BlockSpec(memory_space=pltpu.SMEM)


def vmem():
    return pl.BlockSpec(memory_space=pltpu.VMEM)


def hbm():
    return pl.BlockSpec(memory_space=pl.ANY)


def params(mib):
    return pltpu.CompilerParams(vmem_limit_bytes=mib * 1024 * 1024)


def cost(us, flops=0):
    return pl.CostEstimate(flops=flops, bytes_accessed=int(us * 3.0e6), transcendentals=0)


def lanes(at):
    return pl.ds(pl.multiple_of(at * LANE, LANE), LANE)


ROW, BLOCK, TILE, COLUMN, FIRST, START = range(6)


def plan_kernel(
    chunks, quarter_tiles,
    mine, gen_bus, stor_bus, tile_row, tile_col,
    place, back, sorted_bus, ents,
    tiles,
):
    units = place.shape[0]
    blocks = units // LANE
    kt = tile_row.shape[1]
    square = (LANE, LANE)
    sub = lax.broadcasted_iota(jnp.int32, square, 0).astype(F32)
    lane = lax.broadcasted_iota(jnp.int32, square, 1).astype(F32)
    eye = sub == lane

    def column(row):
        return jnp.sum(jnp.where(eye, jnp.broadcast_to(row, square), 0.0), axis=1, keepdims=True)

    def over_sub(mask, values):
        return jnp.sum(jnp.where(mask, values, 0.0), axis=0, keepdims=True)

    def over_lane(mask, values):
        return jnp.sum(jnp.where(mask, values, 0.0), axis=1, keepdims=True)

    bus = jnp.concatenate([gen_bus[...], stor_bus[...]], axis=1).astype(F32)
    unit = lax.broadcasted_iota(jnp.int32, (1, units), 1).astype(F32)
    key = bus * units + unit
    ordered = jnp.zeros((1, units), F32)
    starts = jnp.zeros((1, LANE), F32)
    stops = jnp.zeros((1, LANE), F32)
    ranks = []
    for b in range(blocks):
        here = column(bus[:, b * LANE : (b + 1) * LANE])
        rank = over_lane(key < here * units + (sub[:, :1] + float(b * LANE)), 1.0)
        mine_at = rank == unit
        place[b * LANE : (b + 1) * LANE] = jnp.where(mine_at, 1.0, 0.0).astype(BF16)
        ordered += over_sub(mine_at, here)
        ranks.append(over_sub(eye, rank))
        starts += over_sub(here < lane * LANE, 1.0)
        stops += over_sub(here < (lane + 1.0) * LANE, 1.0)
    ranks = jnp.concatenate(ranks, axis=1)
    for b in range(blocks):
        back[b * LANE : (b + 1) * LANE] = jnp.where(
            sub[:, :1] + float(b * LANE) == ranks, 1.0, 0.0
        ).astype(BF16)
        sorted_bus[b] = jnp.broadcast_to(column(ordered[:, b * LANE : (b + 1) * LANE]), square)

    tiles[...] = jnp.zeros_like(tiles)
    tiles[0:1, :kt] = tile_row[...]
    tiles[1:2, :kt] = tile_col[...]
    row, col = tiles[0:1], tiles[1:2].astype(F32)
    chunk = jnp.zeros_like(row)
    for d in range(1, chunks):
        chunk = chunk + (row >= d * quarter_tiles).astype(jnp.int32)
    relative = (((chunk ^ mine[0]) - chunk) * quarter_tiles + row).astype(F32)
    number = lane[:1]
    tile_key = jnp.where(number < kt, relative, float(chunks * quarter_tiles)) * LANE + number
    rank = over_sub(column(tile_key) < tile_key, 1.0)
    sorting = rank == sub
    relative, col, tile = (over_lane(sorting, x) for x in (relative, col, number))
    first, last = over_lane(lane == col, starts), over_lane(lane == col, stops)
    block = jnp.minimum(jnp.floor(first * (1.0 / LANE)), float(blocks - 1))
    until = jnp.floor((last - 1.0) * (1.0 / LANE))
    count = jnp.where(last > first, until - block + 1.0, 1.0)
    count = jnp.where(sub[:, :1] < kt, count, 0.0)
    at = over_lane(lane < sub, over_sub(eye, count))
    entry = lax.broadcasted_iota(jnp.int32, (1, ents.shape[1]), 1).astype(F32)
    inside = (at <= entry) & (entry < at + count)
    ents[...] = jnp.zeros_like(ents)
    for name, values in (
        (ROW, relative),
        (BLOCK, block - at + entry),
        (TILE, tile),
        (COLUMN, col),
        (FIRST, (entry == at).astype(F32)),
    ):
        ents[name : name + 1] = over_sub(inside, values).astype(jnp.int32)
    ents[START : START + 1, :LANE] = over_sub(relative < lane * quarter_tiles, count).astype(
        jnp.int32
    )


def sweep(lo, hi, body):
    hi = jnp.maximum(lo, hi)
    long = (hi - lo) // LARGE

    def group(n, _):
        for u in range(LARGE):
            body(lo + n * LARGE + u, None)
        return 0

    lax.fori_loop(0, long, group, 0)
    rest = lo + long * LARGE

    def short(n, _):
        for u in range(SMALL):
            e = rest + n * SMALL + u
            body(e, e < hi)
        return 0

    lax.fori_loop(0, (hi - rest + SMALL - 1) // SMALL, short, 0)


def sweep_held(lo, hi, compact, spill, stage, sem, body):
    kept = compact.shape[0] - SMALL
    sweep(lo, jnp.minimum(hi, kept), lambda e, live: body(e, live, compact.at[e]))

    def fetched(e, _):
        copy = pltpu.make_async_copy(spill.at[e - kept], stage, sem)
        copy.start()
        copy.wait()
        body(e, None, stage)
        return 0

    lax.fori_loop(jnp.maximum(lo, kept), hi, fetched, 0)


def pick(live, value, other):
    return value if live is None else jnp.where(live, value, other)


def build(ents, sorted_bus, load, tiles, compact, spill, base, load_sum, stage, sem, found):
    kept = compact.shape[0] - SMALL
    hours = load.shape[0]
    spare = base.shape[1] // LANE - 1
    base[...] = jnp.zeros_like(base)
    lane = lax.broadcasted_iota(jnp.int32, (LANE, LANE), 1)

    def restricted(e, live):
        col = pick(live, ents[COLUMN, e], 0)
        row = jnp.where(pick(live, ents[FIRST, e], 0) == 1, ents[ROW, e], spare)
        bus = sorted_bus[pick(live, ents[BLOCK, e], 0)]
        hot = jnp.where(bus == (lane + col * LANE).astype(F32), 1.0, 0.0).astype(BF16)
        left = jnp.concatenate([load[:, lanes(col)], hot], axis=0)
        both = mxu(left, tiles[pick(live, ents[TILE, e], 0)], NT)
        base[:, lanes(row)] -= both[:hours]
        return both[hours:].astype(BF16)

    def keep(e, live):
        compact[e] = restricted(e, live)

    def put_out(e, _):
        stage[...] = restricted(e, None)
        copy = pltpu.make_async_copy(stage, spill.at[e - kept], sem)
        copy.start()
        copy.wait()
        return 0

    sweep(jnp.int32(0), jnp.minimum(found, kept), keep)
    lax.fori_loop(jnp.int32(kept), found, put_out, 0)
    total = load[:, :LANE].astype(F32)
    for c in range(1, load.shape[1] // LANE):
        total += load[:, c * LANE : (c + 1) * LANE].astype(F32)
    load_sum[...] = jnp.sum(total, axis=1, keepdims=True)


def add_flows(ents, compact, spill, stage, sem, picked, base, total, cap, chunks, quarter_tiles, first, last, outs):
    origin, width = first * quarter_tiles, (last - first) * quarter_tiles
    total[:, : width * LANE] = base[:, origin * LANE : (origin + width) * LANE]
    spare, blocks = width, picked.shape[0] - 1

    def entry(e, live, matrix):
        row = pick(live, ents[ROW, e] - origin, spare)
        m = pick(live, ents[BLOCK, e], blocks)
        total[:, lanes(row)] += mxu(picked[m], matrix[...], NN)

    lo, hi = ents[START, first], ents[START, last]
    sweep_held(lo, hi, compact, spill, stage, sem, entry)
    for d in range(last - first):
        at = d * quarter_tiles
        outs[d][...] = total[:, at * LANE : (at + quarter_tiles) * LANE].astype(BF16)


def add_prices(
    ents, compact, spill, stage, sem, bars, lines, total, cap, quarter_tiles, first, last
):
    origin, width = first * quarter_tiles, quarter_tiles * LANE
    for d in range(last - first):
        lines[:, d * width : (d + 1) * width] = bars[d][:, :width]
    spare, blocks = (last - first) * quarter_tiles, total.shape[0] - 2

    def entry(e, live, matrix):
        row = pick(live, ents[ROW, e] - origin, spare)
        m = pick(live, ents[BLOCK, e], blocks)
        total[m] += mxu(lines[:, lanes(row)], matrix[...], NT)

    lo, hi = ents[START, first], ents[START, last]
    sweep_held(lo, hi, compact, spill, stage, sem, entry)
    for d in range(last - first):
        total[blocks + 1] += bars[d][:, width:].astype(F32)


def choose(g, p, place, picked):
    x = jnp.concatenate([g.astype(BF16), (-p).astype(BF16)], axis=1)
    chosen = mxu(x, place[...], NN).astype(BF16)
    for m in range(picked.shape[0] - 1):
        picked[m] = chosen[:, m * LANE : (m + 1) * LANE]


def send_hours(g, p, sent):
    hours, stores = p.shape
    gens = g.shape[1]
    sent[:hours] = p
    sent[hours:] = jnp.zeros_like(sent[hours:])
    each = -(-gens // stores)
    for i, row in enumerate((g[:1], g[hours - 1 :])):
        for j in range(each):
            piece = row[:, j * stores : min((j + 1) * stores, gens)]
            sent[hours + i * each + j : hours + i * each + j + 1, : piece.shape[1]] = piece


def own_balance(g, p, load_sum, balance):
    value = jnp.sum(g, axis=1, keepdims=True) - jnp.sum(p, axis=1, keepdims=True) - load_sum[...]
    lane = lax.broadcasted_iota(jnp.int32, balance.shape, 1)
    high = value.astype(BF16).astype(F32)
    middle = (value - high).astype(BF16).astype(F32)
    low = value - high - middle
    balance[...] = jnp.where(
        lane == 0, high, jnp.where(lane == 1, middle, jnp.where(lane == 2, low, 0.0))
    ).astype(BF16)


def first_kernel(
    cap, chunks, quarter_tiles,
    ents, sorted_bus, load, tiles, place, generation, charging,
    compact, spill, base, load_sum, *rest,
):
    upper = chunks - chunks // 2
    outs = rest[:upper]
    balance, sent, picked, stage, sem, total = rest[upper:]
    g, p = generation[...], charging[...]
    send_hours(g, p, sent)
    choose(g, p, place, picked)
    found = ents[START, chunks]
    build(ents, sorted_bus, load, tiles, compact, spill, base, load_sum, stage, sem, found)
    own_balance(g, p, load_sum, balance)
    add_flows(
        ents, compact, spill, stage, sem, picked, base, total,
        cap, chunks, quarter_tiles, chunks // 2, chunks, outs,
    )


def lower_kernel(
    cap, chunks, quarter_tiles, first, last,
    ents, compact, spill, base, picked,
    *rest,
):
    outs = rest[: last - first]
    stage, sem, total = rest[last - first :]
    add_flows(
        ents, compact, spill, stage, sem, picked, base, total,
        cap, chunks, quarter_tiles, first, last, outs,
    )


def price_kernel(cap, quarter_tiles, first, last, fresh, ents, compact, spill, *rest):
    count = last - first
    bars, rest = rest[:count], rest[count:]
    if fresh:
        total, stage, sem, lines = rest
        total[...] = jnp.zeros_like(total)
    else:
        before, total, stage, sem, lines = rest
        total[...] = before[...]
    add_prices(
        ents, compact, spill, stage, sem, bars, lines, total, cap, quarter_tiles, first, last
    )


def step_kernel(
    cap, chunks, quarter_tiles, balance_step, final,
    ents, compact, spill, place, back, before, generation, charging, fixed_g, fixed_p, balance_dual,
    limits, base, load_sum, *rest,
):
    start = chunks - chunks // 4
    count = chunks - start
    bars, rest = rest[:count], rest[count:]
    if final:
        next_g, next_p, stage, sem, lines, prices = rest
    else:
        next_g, next_p, next_balance, *rest = rest
        outs, rest = rest[: chunks - chunks // 2], rest[chunks - chunks // 2 :]
        balance, sent, picked, stage, sem, lines, prices, total = rest
    prices[...] = before[...]
    add_prices(
        ents, compact, spill, stage, sem, bars, lines, prices, cap, quarter_tiles, start, chunks
    )
    hours, gens = generation.shape
    blocks = prices.shape[0] - 2
    price = jnp.concatenate([prices[m] for m in range(blocks)], axis=1)
    high = price.astype(BF16)
    low = (price - high.astype(F32)).astype(BF16)
    price = mxu(jnp.concatenate([high, low], axis=0), back[...], NN)
    price = price[:hours] + price[hours:]
    old = balance_dual[...]
    new = old + balance_step * jnp.sum(prices[blocks + 1], axis=1, keepdims=True)
    bb = 2.0 * new - old
    g = generation[...] - TAU * (bb + price[:, :gens] + fixed_g[...])
    bound = limits[1:2]
    g = jnp.minimum(jnp.maximum(g, 0.0), bound[:, :gens])
    p = charging[...] - TAU * (fixed_p[...] - bb - price[:, gens:])
    p = jnp.minimum(jnp.maximum(p, -bound[:, gens:]), bound[:, gens:])
    next_g[...] = g
    next_p[...] = p
    if not final:
        next_balance[...] = new
        send_hours(g, p, sent)
        own_balance(g, p, load_sum, balance)
        choose(g, p, place, picked)
        add_flows(
            ents, compact, spill, stage, sem, picked, base, total,
            cap, chunks, quarter_tiles, chunks // 2, chunks, outs,
        )


def hourly_kernel(
    years, hours, order,
    where, generation, limits, ramp_dual, state_dual,
    *rest,
):
    heard, rest = rest[:years], rest[years:]
    fixed_g, fixed_p, ramp_out, state_out, everyone, wide, local, bars = rest
    gens = generation.shape[1]
    units = limits.shape[1] - gens
    cost, ramp_limit = limits[0:1, :gens], limits[2:3, :gens]
    cap, keep = limits[2:3, gens:], limits[3:4, gens:]
    each = -(-gens // units)
    me = where[0]
    before = lax.rem(me + years - 1, years)
    after = lax.rem(me + 1, years)
    for j in range(years):
        everyone[me ^ order[j]] = heard[j][...]
    wide[8 : 8 + hours] = generation[...]
    for j in range(each):
        span = min(units, gens - j * units)
        to = slice(j * units, j * units + span)
        at = hours + each + j
        wide[7:8, to] = everyone[before, at : at + 1, :span]
        at = hours + j
        wide[8 + hours : 9 + hours, to] = everyone[after, at : at + 1, :span]
    ramps = wide[8 : 16 + hours] - wide[7 : 15 + hours]
    old = ramp_dual[...]
    shift = old + SIGMA * ramps
    limit = SIGMA * ramp_limit
    new = shift - jnp.minimum(jnp.maximum(shift, -limit), limit)
    ramp_out[...] = new
    wide[0 : 8 + hours] = 2.0 * new - old
    fixed_g[...] = cost + wide[0:hours] - wide[1 : 1 + hours]

    step = lax.broadcasted_iota(jnp.int32, (8, units), 0)
    rise = jnp.exp((step + 1).astype(F32) * keep)
    fall = jnp.exp((8 - step).astype(F32) * keep)
    one, two, four, eight = (jnp.exp(k * keep) for k in (1.0, 2.0, 4.0, 8.0))
    closing = 1.0 / (1.0 - jnp.exp(float(years * hours) * keep))
    count = years * hours // 8
    per = hours // 8

    def within(n, _):
        y = everyone[n // per, pl.ds(pl.multiple_of((n % per) * 8, 8), 8), :]
        for by, factor in ((1, one), (2, two), (4, four)):
            y = y + jnp.where(step >= by, factor * pltpu.roll(y, by, 0), 0.0)
        local[n] = y
        return 0

    lax.fori_loop(0, count, within, 0, unroll=8)
    zero = jnp.zeros((1, units), F32)
    finish = lax.fori_loop(0, count, lambda n, c: local[n][7:8] + eight * c, zero, unroll=8)

    def forward(n, c):
        y = local[n]
        state = y + rise * c
        old = state_dual[n]
        shift = old + SIGMA * state
        new = shift - jnp.minimum(jnp.maximum(shift, 0.0), SIGMA * cap)
        state_out[n] = new
        bar = 2.0 * new - old
        for by, factor in ((1, one), (2, two), (4, four)):
            bar = bar + jnp.where(step < 8 - by, factor * pltpu.roll(bar, 8 - by, 0), 0.0)
        bars[n] = bar
        return y[7:8] + eight * c

    lax.fori_loop(0, count, forward, finish * closing, unroll=8)

    def back(i, c):
        return bars[count - 1 - i][0:1] + eight * c

    finish = lax.fori_loop(0, count, back, zero, unroll=8)
    c = lax.fori_loop(0, count - (me + 1) * per, back, finish * closing)
    for j in reversed(range(per)):
        y = bars[me * per + j]
        fixed_p[8 * j : 8 * j + 8] = y + fall * c
        c = y[0:1] + eight * c


def shards(
    gen_start, charge_start, load, ptdf_tiles, tile_row, tile_col, gen_bus, stor_bus,
    gen_cost, gen_max, ramp_limit, stor_power, stor_loss, stor_cap, flow_limit,
):
    hours, gens = gen_start.shape
    stores = charge_start.shape[1]
    units = gens + stores
    kt = ptdf_tiles.shape[0]
    bus_tiles = load.shape[1] // LANE
    chunks = lax.axis_size("bus")
    years = lax.axis_size("tm")
    lines = flow_limit.shape[0] // chunks
    quarter_tiles = lines // LANE
    blocks = units // LANE
    line_tiles = chunks * quarter_tiles
    mine = lax.axis_index("bus")
    balance_step = SIGMA / (gens * chunks)
    cap = blocks * kt + LARGE
    kept = min(cap, KEPT) // SMALL * SMALL
    sent_rows = -(-(hours + 2 * -(-gens // stores)) // 8) * 8
    groups = years * hours // 8

    def like(*shape, dtype=F32):
        return jax.ShapeDtypeStruct(shape, dtype)

    limits = lax.dynamic_slice_in_dim(flow_limit, mine * lines, lines)[None, :] * SIGMA
    unit_rows = jnp.stack(
        [
            jnp.concatenate([gen_cost, stor_power]),
            jnp.concatenate([gen_max, stor_power]),
            jnp.concatenate([ramp_limit, stor_cap]),
            jnp.concatenate([ramp_limit, jnp.log1p(-stor_loss)]),
        ]
    )

    gen_bus, *early = lax.optimization_barrier((gen_bus, unit_rows, limits))
    unit_rows, limits = early

    width = -(-(cap + SMALL) // LANE) * LANE
    place, back, sorted_bus, ents = pl.pallas_call(
        functools.partial(plan_kernel, chunks, quarter_tiles),
        out_shape=(
            like(units, units, dtype=BF16),
            like(units, units, dtype=BF16),
            like(blocks, LANE, LANE),
            like(8, width, dtype=jnp.int32),
        ),
        in_specs=[smem()] + [vmem()] * 4,
        out_specs=(vmem(),) * 4,
        scratch_shapes=[pltpu.VMEM((8, LANE), jnp.int32)],
        compiler_params=params(STEP_MIB),
        name="plan",
        cost_estimate=cost(3, 3 * 10**9),
    )(
        mine.astype(jnp.int32).reshape(1),
        *[x[None, :] for x in (gen_bus, stor_bus, tile_row, tile_col)],
    )

    chunk_out = (like(hours, lines, dtype=BF16),) * (chunks // 2)
    staging = [pltpu.VMEM((LANE, LANE), BF16), pltpu.SemaphoreType.DMA]
    picked_shape = like(blocks + 1, hours, LANE, dtype=BF16)

    def flow_scratch(count):
        return [pltpu.VMEM((hours, (count * quarter_tiles + 1) * LANE), F32)]

    def line_scratch(count):
        return pltpu.VMEM((hours, (count * quarter_tiles + 1) * LANE), BF16)

    price_shape = (blocks + 2, hours, LANE)
    first_call = pl.pallas_call(
        functools.partial(first_kernel, cap, chunks, quarter_tiles),
        out_shape=(
            like(kept + SMALL, LANE, LANE, dtype=BF16),
            like(max(cap - kept, SPILL), LANE, LANE, dtype=BF16),
            like(hours, (line_tiles + 1) * LANE),
            like(hours, 1),
        )
        + chunk_out
        + (like(hours, LANE, dtype=BF16), like(sent_rows, stores), picked_shape),
        in_specs=[smem()] + [vmem()] * 6,
        out_specs=(vmem(), hbm()) + (vmem(),) * (chunks // 2 + 5),
        scratch_shapes=staging + flow_scratch(chunks // 2),
        compiler_params=params(STEP_MIB),
        name="first",
        cost_estimate=cost(9),
    )

    def lower_call(first, last):
        return pl.pallas_call(
            functools.partial(lower_kernel, cap, chunks, quarter_tiles, first, last),
            out_shape=(like(hours, lines, dtype=BF16),) * (last - first),
            in_specs=[smem(), vmem(), hbm()] + [vmem()] * 2,
            out_specs=(vmem(),) * (last - first),
            scratch_shapes=staging + flow_scratch(last - first),
            compiler_params=params(STEP_MIB),
            name="lower",
            cost_estimate=cost(2),
        )

    def price_call(first, last, fresh):
        return pl.pallas_call(
            functools.partial(price_kernel, cap, quarter_tiles, first, last, fresh),
            out_shape=like(*price_shape),
            in_specs=[smem(), vmem(), hbm()] + [vmem()] * (last - first + (not fresh)),
            out_specs=vmem(),
            scratch_shapes=staging + [line_scratch(last - first)],
            compiler_params=params(STEP_MIB),
            name="price",
            cost_estimate=cost(2),
        )

    tail = chunks - chunks // 4

    def step_call(final):
        shape = (like(hours, gens), like(hours, stores))
        scratch = staging + [line_scratch(chunks - tail), pltpu.VMEM(price_shape, F32)]
        if not final:
            shape += (like(hours, 1),) + chunk_out
            shape += (like(hours, LANE, dtype=BF16), like(sent_rows, stores), picked_shape)
            scratch += flow_scratch(chunks // 2)
        return pl.pallas_call(
            functools.partial(step_kernel, cap, chunks, quarter_tiles, balance_step, final),
            out_shape=shape,
            in_specs=[smem(), vmem(), hbm()] + [vmem()] * (11 + chunks - tail),
            out_specs=(vmem(),) * len(shape),
            scratch_shapes=scratch,
            compiler_params=params(STEP_MIB),
            name="step",
            cost_estimate=cost(4),
        )

    spans = [1 << b for b in reversed(range(years.bit_length() - 1))]
    order = [0]
    for bit in spans:
        order += [j ^ bit for j in order]

    hourly_call = pl.pallas_call(
        functools.partial(hourly_kernel, years, hours, order),
        out_shape=(
            like(hours, gens),
            like(hours, stores),
            like(hours + 8, gens),
            like(groups, 8, stores),
        ),
        in_specs=[smem()] + [vmem()] * (4 + years),
        out_specs=(vmem(),) * 4,
        scratch_shapes=[
            pltpu.VMEM((years, sent_rows, stores), F32),
            pltpu.VMEM((hours + 16, gens), F32),
            pltpu.VMEM((groups, 8, stores), F32),
            pltpu.VMEM((groups, 8, stores), F32),
        ],
        compiler_params=params(STEP_MIB),
        name="hourly",
            cost_estimate=cost(2.4),
    )

    where = lax.axis_index("tm").astype(jnp.int32).reshape(1)
    def swap(x, bit, axis="bus"):
        size = lax.axis_size(axis)
        return lax.ppermute(x, axis, [(i, i ^ bit) for i in range(size)])

    def hear(stacked, over):
        for bit in over:
            stacked = jnp.concatenate([stacked, swap(stacked, bit, "tm")])
        return stacked

    bits = [1 << b for b in range(chunks.bit_length() - 1)]
    line_dual = jnp.zeros((hours, lines), F32)
    ramp_dual = jnp.zeros((hours + 8, gens), F32)
    state_dual = jnp.zeros((groups, 8, stores), F32)
    balance_dual = jnp.zeros((hours, 1), F32)
    g, p = gen_start, charge_start
    compact, spill, base, load_sum, *upper, balance, sent, picked = first_call(
        ents, sorted_bus, load, ptdf_tiles, place, g, p
    )
    half_way = chunks // 2

    def reduce(parts):
        for bit in bits[:-1]:
            for d in sorted(parts, reverse=True):
                if d & bit and not d & (bit - 1):
                    got = swap(sum(x.astype(F32) for x in parts[d]).astype(BF16), bit)
                    parts[d ^ bit].append(got)

    for iteration in range(ITERS):
        parts = {d: [x] for d, x in zip(range(half_way, chunks), upper)}
        reduce(parts)
        ready = sum(x.astype(F32) for x in parts[half_way]).astype(BF16)
        across = swap(ready, half_way)
        parts = {d: [] for d in range(half_way)}
        if half_way > 1:
            made = lower_call(1, half_way)(ents, compact, spill, base, picked)
            for d, x in zip(range(1, half_way), made):
                parts[d].append(x)
        sent, picked, *_ = lax.optimization_barrier((sent, picked, ready))
        parts[0].append(lower_call(0, 1)(ents, compact, spill, base, picked)[0])
        reduce(parts)
        heard = hear(sent[None], spans[:1])
        shift = line_dual + SIGMA * sum(x.astype(F32) for x in parts[0] + [across])
        after = shift - jnp.clip(shift, -limits, limits)
        bar = (2.0 * after - line_dual).astype(BF16)
        line_dual = after
        have = {0: jnp.concatenate([bar, balance], axis=1)}
        heard, have[0] = lax.optimization_barrier((heard, have[0]))
        have[half_way] = swap(have[0], half_way)
        near = [0]
        for bit in reversed(bits[:-1]):
            for d in list(near):
                have[d | bit] = swap(have[d], bit)
                near.append(d | bit)
        prices = price_call(0, half_way, True)(
            ents, compact, spill, *[have[d] for d in range(half_way)]
        )
        heard = hear(heard, spans[1:])
        heard, prices = lax.optimization_barrier((heard, prices))
        fixed_g, fixed_p, ramp_dual, state_dual = hourly_call(
            where, g, unit_rows, ramp_dual, state_dual, *[heard[j] for j in range(years)]
        )
        have[half_way], prices, fixed_g, fixed_p = lax.optimization_barrier(
            (have[half_way], prices, fixed_g, fixed_p)
        )
        far = [half_way]
        for bit in reversed(bits[:-1]):
            for d in list(far):
                have[d | bit] = swap(have[d], bit)
                far.append(d | bit)
        if tail > half_way:
            prices = price_call(half_way, tail, False)(
                ents, compact, spill, *[have[d] for d in range(half_way, tail)], prices
            )
        final = iteration == ITERS - 1
        g, p, *rest = step_call(final)(
            ents, compact, spill, place, back, prices, g, p, fixed_g, fixed_p, balance_dual,
            unit_rows, base, load_sum, *[have[d] for d in range(tail, chunks)],
        )
        if not final:
            balance_dual, *upper, balance, sent, picked = rest
    return g, p, line_dual


STEP_MIB = 16
SPILL = 1500


def solution(mesh):
    rows = P(("scen", "tm"), "bus")
    return jax.shard_map(
        shards,
        mesh=mesh,
        in_specs=(rows, rows, rows, P("bus", None, None)) + (P("bus"),) * 10 + (P(),),
        out_specs=(rows, rows, rows),
        check_vma=False,
    )
```

```python
import functools

import jax
import jax.numpy as jnp
from jax import lax
from jax.experimental import pallas as pl
from jax.experimental.pallas import tpu as pltpu
from jax.sharding import PartitionSpec as P

ITERS = 3
TAU = 0.5
SIGMA = 0.5
LANE = 128
LARGE, SMALL = 32, 8
KEPT = 160
F32 = jnp.float32
BF16 = jnp.bfloat16

NN = (((1,), (0,)), ((), ()))
NT = (((1,), (1,)), ((), ()))


def mxu(a, b, dims):
    return lax.dot_general(a, b, dims, preferred_element_type=F32)


def smem():
    return pl.BlockSpec(memory_space=pltpu.SMEM)


def vmem():
    return pl.BlockSpec(memory_space=pltpu.VMEM)


def hbm():
    return pl.BlockSpec(memory_space=pl.ANY)


def params(mib):
    return pltpu.CompilerParams(vmem_limit_bytes=mib * 1024 * 1024)


def cost(us, flops=0):
    return pl.CostEstimate(flops=flops, bytes_accessed=int(us * 3.0e6), transcendentals=0)


def lanes(at):
    return pl.ds(pl.multiple_of(at * LANE, LANE), LANE)


ROW, BLOCK, START, TILE, COLUMN, FIRST = range(6)
FEW = 256
LOW = 7

COST, HIGH, RAMP, CAP, LOSS = range(5)
BUS, TILES = range(2)


def plan_kernel(
    chunks, quarter_tiles, kt,
    mine, whole,
    place, back, sorted_bus, ents, few,
):
    units = place.shape[0]
    blocks = units // LANE
    square = (LANE, LANE)
    sub = lax.broadcasted_iota(jnp.int32, square, 0).astype(F32)
    lane = lax.broadcasted_iota(jnp.int32, square, 1).astype(F32)
    eye = sub == lane

    def column(row):
        return jnp.sum(jnp.where(eye, jnp.broadcast_to(row, square), 0.0), axis=1, keepdims=True)

    def over_sub(mask, values):
        return jnp.sum(jnp.where(mask, values, 0.0), axis=0, keepdims=True)

    def over_lane(mask, values):
        return jnp.sum(jnp.where(mask, values, 0.0), axis=1, keepdims=True)

    bus = whole[BUS : BUS + 1].astype(F32)
    unit = lax.broadcasted_iota(jnp.int32, (1, units), 1).astype(F32)
    key = bus * units + unit
    ordered = jnp.zeros((1, units), F32)
    starts = jnp.zeros((1, LANE), F32)
    stops = jnp.zeros((1, LANE), F32)
    ranks = []
    for b in range(blocks):
        here = column(bus[:, b * LANE : (b + 1) * LANE])
        rank = over_lane(key < here * units + (sub[:, :1] + float(b * LANE)), 1.0)
        mine_at = rank == unit
        place[b * LANE : (b + 1) * LANE] = jnp.where(mine_at, 1.0, 0.0).astype(BF16)
        ordered += over_sub(mine_at, here)
        ranks.append(over_sub(eye, rank))
        starts += over_sub(here < lane * LANE, 1.0)
        stops += over_sub(here < (lane + 1.0) * LANE, 1.0)
    ranks = jnp.concatenate(ranks, axis=1)
    for b in range(blocks):
        back[b * LANE : (b + 1) * LANE] = jnp.where(
            sub[:, :1] + float(b * LANE) == ranks, 1.0, 0.0
        ).astype(BF16)
        sorted_bus[b] = jnp.broadcast_to(column(ordered[:, b * LANE : (b + 1) * LANE]), square)

    row = whole[TILES : TILES + 1, :LANE]
    col = whole[TILES : TILES + 1, LANE : 2 * LANE].astype(F32)
    chunk = jnp.zeros_like(row)
    for d in range(1, chunks):
        chunk = chunk + (row >= d * quarter_tiles).astype(jnp.int32)
    relative = (((chunk ^ mine[...]) - chunk) * quarter_tiles + row).astype(F32)
    number = lane[:1]
    tile_key = jnp.where(number < kt, relative, float(chunks * quarter_tiles)) * LANE + number
    rank = over_sub(column(tile_key) < tile_key, 1.0)
    sorting = rank == sub
    relative, col, tile = (over_lane(sorting, x) for x in (relative, col, number))
    first, last = over_lane(lane == col, starts), over_lane(lane == col, stops)
    block = jnp.minimum(jnp.floor(first * (1.0 / LANE)), float(blocks - 1))
    until = jnp.floor((last - 1.0) * (1.0 / LANE))
    count = jnp.where(last > first, until - block + 1.0, 1.0)
    count = jnp.where(sub[:, :1] < kt, count, 0.0)
    at = over_lane(lane < sub, over_sub(eye, count))
    entry = lax.broadcasted_iota(jnp.int32, (1, ents.shape[1]), 1).astype(F32)
    inside = (at <= entry) & (entry < at + count)
    ents[...] = jnp.zeros_like(ents)
    for name, values in (
        (ROW, relative),
        (BLOCK, block - at + entry),
        (TILE, tile),
        (COLUMN, col),
        (FIRST, (entry == at).astype(F32)),
    ):
        ents[name : name + 1] = over_sub(inside, values).astype(jnp.int32)
    ents[START : START + 1, :LANE] = over_sub(relative < lane * quarter_tiles, count).astype(
        jnp.int32
    )
    few[...] = ents[: few.shape[0], :FEW]


def sweep(lo, hi, body):
    hi = jnp.maximum(lo, hi)
    long = (hi - lo) // LARGE

    def group(n, _):
        for u in range(LARGE):
            body(lo + n * LARGE + u, None)
        return 0

    lax.fori_loop(0, long, group, 0)
    rest = lo + long * LARGE

    def short(n, _):
        for u in range(SMALL):
            e = rest + n * SMALL + u
            body(e, e < hi)
        return 0

    lax.fori_loop(0, (hi - rest + SMALL - 1) // SMALL, short, 0)


class Lists:
    def __init__(self, few, ents, compact, spill, few_held, ents_held, stage, sems):
        self.ents, self.compact, self.spill = ents, compact, spill
        self.few_held, self.ents_held, self.stage, self.sems = few_held, ents_held, stage, sems
        self.copy = pltpu.make_async_copy(few, few_held, sems.at[0])
        self.copy.start()
        self.kept = compact.shape[0] - SMALL

    def ready(self, chunks):
        self.copy.wait()

        @pl.when(self.few_held[START, chunks] > self.kept)
        def _():
            copy = pltpu.make_async_copy(self.ents, self.ents_held, self.sems.at[1])
            copy.start()
            copy.wait()

    def sweep(self, first, last, body):
        lo, hi = self.few_held[START, first], self.few_held[START, last]
        held, more = self.few_held, self.ents_held
        sweep(
            lo,
            jnp.minimum(hi, self.kept),
            lambda e, live: body(held[ROW, e], held[BLOCK, e], live, self.compact.at[e]),
        )

        def fetched(e, _):
            copy = pltpu.make_async_copy(self.spill.at[e - self.kept], self.stage, self.sems.at[1])
            copy.start()
            copy.wait()
            body(more[ROW, e], more[BLOCK, e], None, self.stage)
            return 0

        lax.fori_loop(jnp.maximum(lo, self.kept), hi, fetched, 0)


def split(x):
    high = x.astype(BF16)
    rest = x - high.astype(F32)
    middle = rest.astype(BF16)
    low = (rest - middle.astype(F32)).astype(BF16)
    return jnp.concatenate([high, middle, low], axis=0)


def joined(x):
    rows = x.shape[0] // 3
    return x[:rows] + x[rows : 2 * rows] + x[2 * rows :]


def pick(live, value, other):
    return value if live is None else jnp.where(live, value, other)


def build(ents, sorted_bus, load, tiles, compact, spill, base, load_sum, stage, sem, found):
    kept = compact.shape[0] - SMALL
    hours = load.shape[0]
    spare = base.shape[1] // LANE - 1
    base[...] = jnp.zeros_like(base)
    lane = lax.broadcasted_iota(jnp.int32, (LANE, LANE), 1)

    def restricted(e, live):
        col = pick(live, ents[COLUMN, e], 0)
        row = jnp.where(pick(live, ents[FIRST, e], 0) == 1, ents[ROW, e], spare)
        bus = sorted_bus[pick(live, ents[BLOCK, e], 0)]
        hot = jnp.where(bus == (lane + col * LANE).astype(F32), 1.0, 0.0).astype(BF16)
        left = jnp.concatenate([load[:, lanes(col)], hot], axis=0)
        both = mxu(left, tiles[pick(live, ents[TILE, e], 0)], NT)
        base[:, lanes(row)] -= both[:hours]
        return both[hours:].astype(BF16)

    def keep(e, live):
        compact[e] = restricted(e, live)

    def put_out(e, _):
        stage[...] = restricted(e, None)
        copy = pltpu.make_async_copy(stage, spill.at[e - kept], sem)
        copy.start()
        copy.wait()
        return 0

    sweep(jnp.int32(0), jnp.minimum(found, kept), keep)
    lax.fori_loop(jnp.int32(kept), found, put_out, 0)
    total = load[:, :LANE].astype(F32)
    for c in range(1, load.shape[1] // LANE):
        total += load[:, c * LANE : (c + 1) * LANE].astype(F32)
    load_sum[...] = jnp.sum(total, axis=1, keepdims=True)


def start_flows(base, total, quarter_tiles, first, last):
    origin, width = first * quarter_tiles, (last - first) * quarter_tiles
    total[:, : width * LANE] = base[:, origin * LANE : (origin + width) * LANE]


def add_flows(lists, picked, total, quarter_tiles, first, last, outs):
    origin, spare, blocks = first * quarter_tiles, (last - first) * quarter_tiles, picked.shape[0] - 1

    def entry(row, m, live, matrix):
        row, m = pick(live, row - origin, spare), pick(live, m, blocks)
        total[:, lanes(row)] += mxu(picked[m], matrix[...], NN)

    lists.sweep(first, last, entry)
    for d in range(last - first):
        at = d * quarter_tiles
        outs[d][...] = total[:, at * LANE : (at + quarter_tiles) * LANE].astype(BF16)


def start_prices(bars, lines, quarter_tiles):
    width = quarter_tiles * LANE
    for d, bar in enumerate(bars):
        lines[:, d * width : (d + 1) * width] = bar[:, :width]


def add_prices(lists, bars, lines, total, quarter_tiles, first, last):
    origin, width = first * quarter_tiles, quarter_tiles * LANE
    spare, blocks = (last - first) * quarter_tiles, total.shape[0] - 2

    def entry(row, m, live, matrix):
        row, m = pick(live, row - origin, spare), pick(live, m, blocks)
        total[m] += mxu(lines[:, lanes(row)], matrix[...], NT)

    lists.sweep(first, last, entry)
    for bar in bars:
        total[blocks + 1] += bar[:, width:].astype(F32)


def put_picked(z, picked):
    for m in range(picked.shape[0] - 1):
        picked[m] = z[:, m * LANE : (m + 1) * LANE].astype(BF16)


def send_hours(z, own, sent):
    hours, units = z.shape
    stores = own.shape[1]
    sent[:hours] = own
    sent[hours:] = jnp.zeros_like(sent[hours:])
    each = -(-units // stores)
    for i, row in enumerate((z[:1], z[hours - 1 :])):
        for j in range(each):
            piece = row[:, j * stores : min((j + 1) * stores, units)]
            sent[hours + i * each + j : hours + i * each + j + 1, : piece.shape[1]] = piece


def own_balance(z, load_sum, balance):
    value = jnp.sum(z, axis=1, keepdims=True) - load_sum[...]
    lane = lax.broadcasted_iota(jnp.int32, balance.shape, 1)
    high = value.astype(BF16).astype(F32)
    middle = (value - high).astype(BF16).astype(F32)
    low = value - high - middle
    balance[...] = jnp.where(
        lane == 0, high, jnp.where(lane == 1, middle, jnp.where(lane == 2, low, 0.0))
    ).astype(BF16)


def first_kernel(
    chunks, quarter_tiles,
    few, ents, pars, sorted_bus, load, tiles, place, generation, charging,
    compact, spill, base, load_sum, state, rows, *rest,
):
    upper = chunks - chunks // 2
    outs = rest[:upper]
    balance, picked, few_held, ents_held, stage, sems, total = rest[upper:]
    copy = pltpu.make_async_copy(ents, ents_held, sems.at[2])
    copy.start()
    lists = Lists(few, ents, compact, spill, few_held, ents_held, stage, sems)
    hours, gens = generation.shape
    x = jnp.concatenate([generation[...], -charging[...]], axis=1)
    unit = lax.broadcasted_iota(jnp.int32, pars.shape, 1)
    name = lax.broadcasted_iota(jnp.int32, pars.shape, 0)
    own = pars[...]
    low = jnp.broadcast_to(jnp.where(unit[:1] < gens, 0.0, -own[HIGH : HIGH + 1]), own.shape)
    own = jnp.where(name == LOW, low, own)
    own = jnp.where((name == RAMP) & (unit >= gens), 1e30, own)
    left = jnp.concatenate([split(x), split(own)], axis=0)
    ordered = mxu(left, place[...], NN)
    z = joined(ordered[: 3 * hours])
    state[...] = z
    rows[...] = joined(ordered[3 * hours :])
    put_picked(z, picked)
    copy.wait()
    found = ents_held[START, chunks]
    build(ents_held, sorted_bus, load, tiles, compact, spill, base, load_sum, stage, sems.at[1], found)
    own_balance(z, load_sum, balance)
    lists.ready(chunks)
    start_flows(base, total, quarter_tiles, chunks // 2, chunks)
    add_flows(lists, picked, total, quarter_tiles, chunks // 2, chunks, outs)


def lower_kernel(
    chunks, quarter_tiles, first, last,
    few, ents, compact, spill, base, picked, state, back,
    *rest,
):
    outs, rest = rest[: last - first], rest[last - first :]
    if first:
        sent, rest = rest[0], rest[1:]
    few_held, ents_held, stage, sems, total = rest
    lists = Lists(few, ents, compact, spill, few_held, ents_held, stage, sems)
    start_flows(base, total, quarter_tiles, first, last)
    if first:
        z = state[...]
        stores = sent.shape[1]
        own = -joined(mxu(split(z), back[:, z.shape[1] - stores :], NN))
        send_hours(z, own, sent)
    lists.ready(chunks)
    add_flows(lists, picked, total, quarter_tiles, first, last, outs)


def price_kernel(
    chunks, quarter_tiles, first, last, fresh,
    few, ents, compact, spill, *rest,
):
    bars, rest = rest[: last - first], rest[last - first :]
    if not fresh:
        before, rest = rest[0], rest[1:]
    total, few_held, ents_held, stage, sems, lines = rest
    lists = Lists(few, ents, compact, spill, few_held, ents_held, stage, sems)
    total[...] = jnp.zeros_like(total) if fresh else before[...]
    start_prices(bars, lines, quarter_tiles)
    lists.ready(chunks)
    add_prices(lists, bars, lines, total, quarter_tiles, first, last)


def step_kernel(
    chunks, quarter_tiles, balance_step, final,
    few, ents, compact, spill, before, state, fixed, balance_dual, rows, base, load_sum, back,
    *rest,
):
    start, upper = chunks - chunks // 4, chunks // 2
    bars, rest = rest[: chunks - start], rest[chunks - start :]
    if final:
        next_g, next_p, few_held, ents_held, stage, sems, lines, prices = rest
    else:
        next_state, next_balance, *rest = rest
        outs, rest = rest[: chunks - upper], rest[chunks - upper :]
        balance, picked, few_held, ents_held, stage, sems, lines, prices, total = rest
    lists = Lists(few, ents, compact, spill, few_held, ents_held, stage, sems)
    prices[...] = before[...]
    start_prices(bars, lines, quarter_tiles)
    if not final:
        start_flows(base, total, quarter_tiles, upper, chunks)
    lists.ready(chunks)
    add_prices(lists, bars, lines, prices, quarter_tiles, start, chunks)
    blocks = prices.shape[0] - 2
    price = jnp.concatenate([prices[m] for m in range(blocks)], axis=1)
    old = balance_dual[...]
    new = old + balance_step * jnp.sum(prices[blocks + 1], axis=1, keepdims=True)
    bb = 2.0 * new - old
    high = rows[HIGH : HIGH + 1]
    z = state[...] - TAU * (bb + price + fixed[...])
    z = jnp.minimum(jnp.maximum(z, rows[LOW : LOW + 1]), high)
    if final:
        gens = next_g.shape[1]
        x = joined(mxu(split(z), back[...], NN))
        next_g[...] = x[:, :gens]
        next_p[...] = -x[:, gens:]
    else:
        next_state[...] = z
        next_balance[...] = new
        own_balance(z, load_sum, balance)
        put_picked(z, picked)
        add_flows(lists, picked, total, quarter_tiles, upper, chunks, outs)


def hourly_kernel(
    years, hours, order, final,
    where, state, rows, pars, place, ramp_dual, state_dual,
    *rest,
):
    heard, rest = rest[:years], rest[years:]
    if final:
        fixed, everyone, wide, local, bars, adjoint = rest
    else:
        fixed, ramp_out, state_out, everyone, wide, local, bars, adjoint = rest
    gens = state.shape[1]
    units = adjoint.shape[1]
    cost, ramp_limit = rows[COST : COST + 1], rows[RAMP : RAMP + 1]
    cap = pars[CAP : CAP + 1, gens - units :]
    keep = jnp.log1p(-pars[LOSS : LOSS + 1, gens - units :])
    each = -(-gens // units)
    me = where[0]
    before = lax.rem(me + years - 1, years)
    after = lax.rem(me + 1, years)
    for j in range(years):
        everyone[me ^ order[j]] = heard[j][...]
    wide[8 : 8 + hours] = state[...]
    for j in range(each):
        span = min(units, gens - j * units)
        to = slice(j * units, j * units + span)
        at = hours + each + j
        wide[7:8, to] = everyone[before, at : at + 1, :span]
        at = hours + j
        wide[8 + hours : 9 + hours, to] = everyone[after, at : at + 1, :span]
    ramps = wide[8 : 16 + hours] - wide[7 : 15 + hours]
    old = ramp_dual[...]
    shift = old + SIGMA * ramps
    limit = SIGMA * ramp_limit
    new = shift - jnp.minimum(jnp.maximum(shift, -limit), limit)
    if not final:
        ramp_out[...] = new
    wide[0 : 8 + hours] = 2.0 * new - old
    fixed[...] = cost + wide[0:hours] - wide[1 : 1 + hours]

    step = lax.broadcasted_iota(jnp.int32, (8, units), 0)
    rise = jnp.exp((step + 1).astype(F32) * keep)
    fall = jnp.exp((8 - step).astype(F32) * keep)
    one, two, four, eight = (jnp.exp(k * keep) for k in (1.0, 2.0, 4.0, 8.0))
    closing = 1.0 / (1.0 - jnp.exp(float(years * hours) * keep))
    count = years * hours // 8
    per = hours // 8

    def within(n, _):
        y = everyone[n // per, pl.ds(pl.multiple_of((n % per) * 8, 8), 8), :]
        for by, factor in ((1, one), (2, two), (4, four)):
            y = y + jnp.where(step >= by, factor * pltpu.roll(y, by, 0), 0.0)
        local[n] = y
        return 0

    lax.fori_loop(0, count, within, 0, unroll=8)
    zero = jnp.zeros((1, units), F32)
    finish = lax.fori_loop(0, count, lambda n, c: local[n][7:8] + eight * c, zero, unroll=8)

    def forward(n, c):
        y = local[n]
        state = y + rise * c
        old = state_dual[n]
        shift = old + SIGMA * state
        new = shift - jnp.minimum(jnp.maximum(shift, 0.0), SIGMA * cap)
        if not final:
            state_out[n] = new
        bar = 2.0 * new - old
        for by, factor in ((1, one), (2, two), (4, four)):
            bar = bar + jnp.where(step < 8 - by, factor * pltpu.roll(bar, 8 - by, 0), 0.0)
        bars[n] = bar
        return y[7:8] + eight * c

    lax.fori_loop(0, count, forward, finish * closing, unroll=8)

    def back(i, c):
        return bars[count - 1 - i][0:1] + eight * c

    finish = lax.fori_loop(0, count, back, zero, unroll=8)
    c = lax.fori_loop(0, count - (me + 1) * per, back, finish * closing)
    for j in reversed(range(per)):
        y = bars[me * per + j]
        adjoint[8 * j : 8 * j + 8] = y + fall * c
        c = y[0:1] + eight * c
    fixed[...] -= joined(mxu(split(adjoint[...]), place[gens - units :], NN))


def shards(
    gen_start, charge_start, load, ptdf_tiles, tile_row, tile_col, gen_bus, stor_bus,
    gen_cost, gen_max, ramp_limit, stor_power, stor_loss, stor_cap, flow_limit,
):
    hours, gens = gen_start.shape
    stores = charge_start.shape[1]
    units = gens + stores
    kt = ptdf_tiles.shape[0]
    bus_tiles = load.shape[1] // LANE
    chunks = lax.axis_size("bus")
    years = lax.axis_size("tm")
    lines = flow_limit.shape[0] // chunks
    quarter_tiles = lines // LANE
    blocks = units // LANE
    line_tiles = chunks * quarter_tiles
    mine = lax.axis_index("bus")
    balance_step = SIGMA / (gens * chunks)
    cap = blocks * kt + LARGE
    kept = min(cap, KEPT) // SMALL * SMALL
    sent_rows = -(-(hours + 2 * -(-units // stores)) // 8) * 8
    groups = years * hours // 8

    def like(*shape, dtype=F32):
        return jax.ShapeDtypeStruct(shape, dtype)


    def placed(count, *parts):
        total = 0
        for row, at, x in parts:
            before = row * units + at
            total += jnp.pad(x, (before, count * units - before - x.shape[0]))
        return total.reshape(count, units)

    pars = placed(
        8,
        (COST, 0, gen_cost),
        (HIGH, 0, gen_max),
        (HIGH, gens, stor_power),
        (RAMP, 0, ramp_limit),
        (CAP, gens, stor_cap),
        (LOSS, gens, stor_loss),
    )
    whole = placed(
        2, (BUS, 0, gen_bus), (BUS, gens, stor_bus), (TILES, 0, tile_row), (TILES, LANE, tile_col)
    )

    width = -(-(cap + SMALL) // LANE) * LANE
    where = lax.axis_index("tm").astype(jnp.int32).reshape(1)
    from_line = mine.astype(jnp.uint32) * lines
    whole, where, from_line = lax.optimization_barrier((whole, where, from_line))
    place, back, sorted_bus, ents, few = pl.pallas_call(
        functools.partial(plan_kernel, chunks, quarter_tiles, kt),
        out_shape=(
            like(units, units, dtype=BF16),
            like(units, units, dtype=BF16),
            like(blocks, LANE, LANE),
            like(8, width, dtype=jnp.int32),
            like(4, FEW, dtype=jnp.int32),
        ),
        in_specs=[vmem()] * 2,
        out_specs=(vmem(),) * 5,
        compiler_params=params(STEP_MIB),
        name="plan",
        cost_estimate=cost(3, 3 * 10**9),
    )(jnp.broadcast_to(mine.astype(jnp.int32), (1, LANE)), whole)

    chunk_out = (like(hours, lines, dtype=BF16),) * (chunks // 2)
    staging = [
        pltpu.SMEM((4, FEW), jnp.int32),
        pltpu.SMEM((8, width), jnp.int32),
        pltpu.VMEM((LANE, LANE), BF16),
        pltpu.SemaphoreType.DMA((3,)),
    ]
    lists = [vmem(), vmem(), vmem(), hbm()]
    picked_shape = like(blocks + 1, hours, LANE, dtype=BF16)

    def flow_scratch(count):
        return [pltpu.VMEM((hours, (count * quarter_tiles + 1) * LANE), F32)]

    def line_scratch(count):
        return pltpu.VMEM((hours, (count * quarter_tiles + 1) * LANE), BF16)

    price_shape = (blocks + 2, hours, LANE)
    first_call = pl.pallas_call(
        functools.partial(first_kernel, chunks, quarter_tiles),
        out_shape=(
            like(kept + SMALL, LANE, LANE, dtype=BF16),
            like(max(cap - kept, SPILL), LANE, LANE, dtype=BF16),
            like(hours, (line_tiles + 1) * LANE),
            like(hours, 1),
            like(hours, units),
            like(8, units),
        )
        + chunk_out
        + (like(hours, LANE, dtype=BF16), picked_shape),
        in_specs=[vmem()] * 9,
        out_specs=(vmem(), hbm()) + (vmem(),) * (chunks // 2 + 6),
        scratch_shapes=staging + flow_scratch(chunks // 2),
        compiler_params=params(STEP_MIB),
        name="first",
        cost_estimate=cost(9),
    )

    def lower_call(first, last):
        return pl.pallas_call(
            functools.partial(lower_kernel, chunks, quarter_tiles, first, last),
            out_shape=(like(hours, lines, dtype=BF16),) * (last - first)
            + ((like(sent_rows, stores),) if first else ()),
            in_specs=lists + [vmem()] * 4,
            out_specs=(vmem(),) * (last - first + (first > 0)),
            scratch_shapes=staging + flow_scratch(last - first),
            compiler_params=params(STEP_MIB),
            name="lower",
            cost_estimate=cost(2),
        )

    def line_scratch(count):
        return pltpu.VMEM((hours, (count * quarter_tiles + 1) * LANE), BF16)

    price_shape = (blocks + 2, hours, LANE)

    def price_call(first, last, fresh):
        return pl.pallas_call(
            functools.partial(price_kernel, chunks, quarter_tiles, first, last, fresh),
            out_shape=like(*price_shape),
            in_specs=lists + [vmem()] * (last - first + (not fresh)),
            out_specs=vmem(),
            scratch_shapes=staging + [line_scratch(last - first)],
            compiler_params=params(STEP_MIB),
            name="price",
            cost_estimate=cost(2),
        )

    tail = chunks - chunks // 4

    def step_call(final):
        scratch = staging + [line_scratch(chunks - tail), pltpu.VMEM(price_shape, F32)]
        if final:
            shape = (like(hours, gens), like(hours, stores))
        else:
            shape = (like(hours, units), like(hours, 1)) + chunk_out
            shape += (like(hours, LANE, dtype=BF16), picked_shape)
            scratch += flow_scratch(chunks // 2)
        return pl.pallas_call(
            functools.partial(step_kernel, chunks, quarter_tiles, balance_step, final),
            out_shape=shape,
            in_specs=lists + [vmem()] * (8 + chunks - tail),
            out_specs=(vmem(),) * len(shape),
            scratch_shapes=scratch,
            compiler_params=params(STEP_MIB),
            name="step",
            cost_estimate=cost(4),
        )

    spans = [1 << b for b in reversed(range(years.bit_length() - 1))]
    order = [0]
    for bit in spans:
        order += [j ^ bit for j in order]

    def hourly_call(final):
        shape = (like(hours, units),)
        if not final:
            shape += (like(hours + 8, units), like(groups, 8, stores))
        return pl.pallas_call(
            functools.partial(hourly_kernel, years, hours, order, final),
            out_shape=shape,
            in_specs=[smem()] + [vmem()] * (6 + years),
            out_specs=(vmem(),) * len(shape),
            scratch_shapes=[
                pltpu.VMEM((years, sent_rows, stores), F32),
                pltpu.VMEM((hours + 16, units), F32),
                pltpu.VMEM((groups, 8, stores), F32),
                pltpu.VMEM((groups, 8, stores), F32),
                pltpu.VMEM((hours, stores), F32),
            ],
            compiler_params=params(STEP_MIB),
            name="hourly",
            cost_estimate=cost(2.4),
        )

    def swap(x, bit, axis="bus"):
        size = lax.axis_size(axis)
        return lax.ppermute(x, axis, [(i, i ^ bit) for i in range(size)])

    def hear(stacked, over):
        for bit in over:
            stacked = jnp.concatenate([stacked, swap(stacked, bit, "tm")])
        return stacked

    bits = [1 << b for b in range(chunks.bit_length() - 1)]
    line_dual = jnp.zeros((hours, lines), F32)
    ramp_dual = jnp.zeros((hours + 8, units), F32)
    state_dual = jnp.zeros((groups, 8, stores), F32)
    balance_dual = jnp.zeros((hours, 1), F32)
    compact, spill, base, load_sum, state, unit_rows, *upper, balance, picked = first_call(
        few, ents, pars, sorted_bus, load, ptdf_tiles, place, gen_start, charge_start
    )
    held = (few, ents, compact, spill)
    half_way = chunks // 2

    def reduce(parts):
        for bit in bits[:-1]:
            for d in sorted(parts, reverse=True):
                if d & bit and not d & (bit - 1):
                    got = swap(sum(x.astype(F32) for x in parts[d]).astype(BF16), bit)
                    parts[d ^ bit].append(got)

    for iteration in range(ITERS):
        parts = {d: [x] for d, x in zip(range(half_way, chunks), upper)}
        reduce(parts)
        ready = sum(x.astype(F32) for x in parts[half_way]).astype(BF16)
        across = swap(ready, half_way)
        parts = {d: [] for d in range(half_way)}
        *made, sent = lower_call(1, half_way)(*held, base, picked, state, back)
        for d, x in zip(range(1, half_way), made):
            parts[d].append(x)
        sent, picked, *_ = lax.optimization_barrier((sent, picked, ready))
        parts[0].append(lower_call(0, 1)(*held, base, picked, state, back)[0])
        reduce(parts)
        heard = hear(sent[None], spans[:1])
        limits = SIGMA * lax.dynamic_slice(flow_limit, (from_line,), (lines,))
        shift = line_dual + SIGMA * sum(x.astype(F32) for x in parts[0] + [across])
        after = shift - jnp.clip(shift, -limits, limits)
        bar = (2.0 * after - line_dual).astype(BF16)
        line_dual = after
        have = {0: jnp.concatenate([bar, balance], axis=1)}
        heard, have[0] = lax.optimization_barrier((heard, have[0]))
        have[half_way] = swap(have[0], half_way)
        near = [0]
        for bit in reversed(bits[:-1]):
            for d in list(near):
                have[d | bit] = swap(have[d], bit)
                near.append(d | bit)
        final = iteration == ITERS - 1
        heard = hear(heard, spans[1:])
        fixed, *duals = hourly_call(final)(
            where, state, unit_rows, pars, place, ramp_dual, state_dual,
            *[heard[j] for j in range(years)],
        )
        have[0], fixed = lax.optimization_barrier((have[0], fixed))
        prices = price_call(0, half_way, True)(*held, *[have[d] for d in range(half_way)])
        have[half_way], prices, fixed = lax.optimization_barrier((have[half_way], prices, fixed))
        far = [half_way]
        for bit in reversed(bits[:-1]):
            for d in list(far):
                have[d | bit] = swap(have[d], bit)
                far.append(d | bit)
        if tail > half_way:
            prices = price_call(half_way, tail, False)(
                *held, *[have[d] for d in range(half_way, tail)], prices
            )
        made = step_call(final)(
            *held, prices, state, fixed, balance_dual, unit_rows, base, load_sum, back,
            *[have[d] for d in range(tail, chunks)],
        )
        if not final:
            ramp_dual, state_dual = duals
            state, balance_dual, *upper, balance, picked = made
    return *made, line_dual


STEP_MIB = 16
SPILL = 1500


def solution(mesh):
    rows = P(("scen", "tm"), "bus")
    return jax.shard_map(
        shards,
        mesh=mesh,
        in_specs=(rows, rows, rows, P("bus", None, None)) + (P("bus"),) * 10 + (P(),),
        out_specs=(rows, rows, rows),
        check_vma=False,
    )
```

```python
import functools

import jax
import jax.numpy as jnp
from jax import lax
from jax.experimental import pallas as pl
from jax.experimental.pallas import tpu as pltpu
from jax.sharding import PartitionSpec as P

ITERS = 3
TAU = 0.5
SIGMA = 0.5
LANE = 128
GROUPS = (64, 32, 8)
LARGE, SMALL = GROUPS[0], GROUPS[-1]
KEPT = 160
F32 = jnp.float32
BF16 = jnp.bfloat16

NN = (((1,), (0,)), ((), ()))
NT = (((1,), (1,)), ((), ()))


def mxu(a, b, dims):
    return lax.dot_general(a, b, dims, preferred_element_type=F32)


def smem():
    return pl.BlockSpec(memory_space=pltpu.SMEM)


def vmem():
    return pl.BlockSpec(memory_space=pltpu.VMEM)


def hbm():
    return pl.BlockSpec(memory_space=pl.ANY)


def params(mib):
    return pltpu.CompilerParams(vmem_limit_bytes=mib * 1024 * 1024)


def cost(us, flops=0):
    return pl.CostEstimate(flops=flops, bytes_accessed=int(us * 3.0e6), transcendentals=0)


def lanes(at):
    return pl.ds(pl.multiple_of(at * LANE, LANE), LANE)


ROW, BLOCK, START, TILE, COLUMN, FIRST = range(6)
FEW = 256
LOW = 7

COST, HIGH, RAMP, CAP, LOSS = range(5)
BUS, TILES = range(2)


def plan_kernel(
    chunks, quarter_tiles, kt,
    mine, whole,
    place, back, sorted_bus, ents, few,
):
    units = place.shape[0]
    blocks = units // LANE
    square = (LANE, LANE)
    sub = lax.broadcasted_iota(jnp.int32, square, 0).astype(F32)
    lane = lax.broadcasted_iota(jnp.int32, square, 1).astype(F32)
    eye = sub == lane

    def column(row):
        return jnp.sum(jnp.where(eye, jnp.broadcast_to(row, square), 0.0), axis=1, keepdims=True)

    def over_sub(mask, values):
        return jnp.sum(jnp.where(mask, values, 0.0), axis=0, keepdims=True)

    def over_lane(mask, values):
        return jnp.sum(jnp.where(mask, values, 0.0), axis=1, keepdims=True)

    bus = whole[BUS : BUS + 1].astype(F32)
    unit = lax.broadcasted_iota(jnp.int32, (1, units), 1).astype(F32)
    key = bus * units + unit
    ordered = jnp.zeros((1, units), F32)
    starts = jnp.zeros((1, LANE), F32)
    stops = jnp.zeros((1, LANE), F32)
    ranks = []
    for b in range(blocks):
        here = column(bus[:, b * LANE : (b + 1) * LANE])
        rank = over_lane(key < here * units + (sub[:, :1] + float(b * LANE)), 1.0)
        mine_at = rank == unit
        place[b * LANE : (b + 1) * LANE] = jnp.where(mine_at, 1.0, 0.0).astype(BF16)
        ordered += over_sub(mine_at, here)
        ranks.append(over_sub(eye, rank))
        starts += over_sub(here < lane * LANE, 1.0)
        stops += over_sub(here < (lane + 1.0) * LANE, 1.0)
    ranks = jnp.concatenate(ranks, axis=1)
    for b in range(blocks):
        back[b * LANE : (b + 1) * LANE] = jnp.where(
            sub[:, :1] + float(b * LANE) == ranks, 1.0, 0.0
        ).astype(BF16)
        sorted_bus[b] = jnp.broadcast_to(column(ordered[:, b * LANE : (b + 1) * LANE]), square)

    row = whole[TILES : TILES + 1, :LANE]
    col = whole[TILES : TILES + 1, LANE : 2 * LANE].astype(F32)
    chunk = jnp.zeros_like(row)
    for d in range(1, chunks):
        chunk = chunk + (row >= d * quarter_tiles).astype(jnp.int32)
    relative = chunk ^ mine[...]
    half = chunks // 2
    slot = 2 * (relative & (half - 1)) + (relative >= half).astype(jnp.int32)
    relative = ((slot - chunk) * quarter_tiles + row).astype(F32)
    number = lane[:1]
    tile_key = jnp.where(number < kt, relative, float(chunks * quarter_tiles)) * LANE + number
    rank = over_sub(column(tile_key) < tile_key, 1.0)
    sorting = rank == sub
    relative, col, tile = (over_lane(sorting, x) for x in (relative, col, number))
    first, last = over_lane(lane == col, starts), over_lane(lane == col, stops)
    block = jnp.minimum(jnp.floor(first * (1.0 / LANE)), float(blocks - 1))
    until = jnp.floor((last - 1.0) * (1.0 / LANE))
    count = jnp.where(last > first, until - block + 1.0, 1.0)
    count = jnp.where(sub[:, :1] < kt, count, 0.0)
    at = over_lane(lane < sub, over_sub(eye, count))
    entry = lax.broadcasted_iota(jnp.int32, (1, ents.shape[1]), 1).astype(F32)
    inside = (at <= entry) & (entry < at + count)
    ents[...] = jnp.zeros_like(ents)
    for name, values in (
        (ROW, relative),
        (BLOCK, block - at + entry),
        (TILE, tile),
        (COLUMN, col),
        (FIRST, (entry == at).astype(F32)),
    ):
        ents[name : name + 1] = over_sub(inside, values).astype(jnp.int32)
    ents[START : START + 1, :LANE] = over_sub(relative < lane * quarter_tiles, count).astype(
        jnp.int32
    )
    few[...] = ents[: few.shape[0], :FEW]


def sweep(lo, hi, body):
    hi = jnp.maximum(lo, hi)
    for size in GROUPS[:-1]:

        def group(n, _, size=size, lo=lo):
            for u in range(size):
                body(lo + n * size + u, None)
            return 0

        count = (hi - lo) // size
        lax.fori_loop(0, count, group, 0)
        lo = lo + count * size

    def short(n, _):
        for u in range(SMALL):
            e = lo + n * SMALL + u
            body(e, e < hi)
        return 0

    lax.fori_loop(0, (hi - lo + SMALL - 1) // SMALL, short, 0)


class Lists:
    def __init__(self, few, ents, compact, spill, few_held, ents_held, stage, sems):
        self.ents, self.compact, self.spill = ents, compact, spill
        self.few_held, self.ents_held, self.stage, self.sems = few_held, ents_held, stage, sems
        self.copy = pltpu.make_async_copy(few, few_held, sems.at[0])
        self.copy.start()
        self.kept = compact.shape[0] - SMALL

    def ready(self, chunks):
        self.copy.wait()

        @pl.when(self.few_held[START, chunks] > self.kept)
        def _():
            copy = pltpu.make_async_copy(self.ents, self.ents_held, self.sems.at[1])
            copy.start()
            copy.wait()

    def sweep(self, first, last, body):
        lo, hi = self.few_held[START, first], self.few_held[START, last]
        held, more = self.few_held, self.ents_held
        sweep(
            lo,
            jnp.minimum(hi, self.kept),
            lambda e, live: body(held[ROW, e], held[BLOCK, e], live, self.compact.at[e]),
        )

        def fetched(e, _):
            copy = pltpu.make_async_copy(self.spill.at[e - self.kept], self.stage, self.sems.at[1])
            copy.start()
            copy.wait()
            body(more[ROW, e], more[BLOCK, e], None, self.stage)
            return 0

        lax.fori_loop(jnp.maximum(lo, self.kept), hi, fetched, 0)


def split(x):
    high = x.astype(BF16)
    rest = x - high.astype(F32)
    middle = rest.astype(BF16)
    low = (rest - middle.astype(F32)).astype(BF16)
    return jnp.concatenate([high, middle, low], axis=0)


def joined(x):
    rows = x.shape[0] // 3
    return x[:rows] + x[rows : 2 * rows] + x[2 * rows :]


def pick(live, value, other):
    return value if live is None else jnp.where(live, value, other)


def build(ents, sorted_bus, load, tiles, compact, spill, base, load_sum, stage, sem, found):
    kept = compact.shape[0] - SMALL
    hours = load.shape[0]
    spare = base.shape[1] // LANE - 1
    base[...] = jnp.zeros_like(base)
    lane = lax.broadcasted_iota(jnp.int32, (LANE, LANE), 1)

    def restricted(e, live):
        col = pick(live, ents[COLUMN, e], 0)
        row = jnp.where(pick(live, ents[FIRST, e], 0) == 1, ents[ROW, e], spare)
        bus = sorted_bus[pick(live, ents[BLOCK, e], 0)]
        hot = jnp.where(bus == (lane + col * LANE).astype(F32), 1.0, 0.0).astype(BF16)
        left = jnp.concatenate([load[:, lanes(col)], hot], axis=0)
        both = mxu(left, tiles[pick(live, ents[TILE, e], 0)], NT)
        base[:, lanes(row)] -= both[:hours]
        return both[hours:].astype(BF16)

    def keep(e, live):
        compact[e] = restricted(e, live)

    def put_out(e, _):
        stage[...] = restricted(e, None)
        copy = pltpu.make_async_copy(stage, spill.at[e - kept], sem)
        copy.start()
        copy.wait()
        return 0

    sweep(jnp.int32(0), jnp.minimum(found, kept), keep)
    lax.fori_loop(jnp.int32(kept), found, put_out, 0)
    total = load[:, :LANE].astype(F32)
    for c in range(1, load.shape[1] // LANE):
        total += load[:, c * LANE : (c + 1) * LANE].astype(F32)
    load_sum[...] = jnp.sum(total, axis=1, keepdims=True)


def start_flows(base, total, quarter_tiles, first, last):
    width = 2 * quarter_tiles * LANE
    total[:, : (last - first) * width] = base[:, first * width : last * width]


def add_flows(lists, picked, total, balance, quarter_tiles, first, last, outs):
    width = quarter_tiles * LANE
    origin, spare = 2 * first * quarter_tiles, 2 * (last - first) * quarter_tiles
    blocks = picked.shape[0] - 1

    def entry(row, m, live, matrix):
        row, m = pick(live, row - origin, spare), pick(live, m, blocks)
        total[:, lanes(row)] += mxu(picked[m], matrix[...], NN)

    lists.sweep(2 * first, 2 * last, entry)
    for d, out in enumerate(outs):
        at = 2 * d * width
        out[:, :width] = total[:, at : at + width].astype(BF16)
        out[:, width : width + LANE] = balance
        out[:, width + LANE :] = total[:, at + width : at + 2 * width].astype(BF16)


def start_prices(bars, lines, quarter_tiles):
    width = quarter_tiles * LANE
    for d, bar in enumerate(bars):
        lines[:, d * width : (d + 1) * width] = bar[...]


def add_prices(lists, lines, total, quarter_tiles, first, last):
    origin = first * quarter_tiles
    spare, blocks = (last - first) * quarter_tiles, total.shape[0] - 1

    def entry(row, m, live, matrix):
        row, m = pick(live, row - origin, spare), pick(live, m, blocks)
        total[m] += mxu(lines[:, lanes(row)], matrix[...], NT)

    lists.sweep(first, last, entry)


def put_picked(z, picked):
    for m in range(picked.shape[0] - 1):
        picked[m] = z[:, m * LANE : (m + 1) * LANE].astype(BF16)


def send_hours(z, own, sent):
    hours, units = z.shape
    stores = own.shape[1]
    sent[:hours] = own
    sent[hours:] = jnp.zeros_like(sent[hours:])
    each = -(-units // stores)
    for i, row in enumerate((z[:1], z[hours - 1 :])):
        for j in range(each):
            piece = row[:, j * stores : min((j + 1) * stores, units)]
            sent[hours + i * each + j : hours + i * each + j + 1, : piece.shape[1]] = piece


def own_balance(z, load_sum, mine):
    value = jnp.sum(z, axis=1, keepdims=True) - load_sum[...]
    lane = lax.broadcasted_iota(jnp.int32, (z.shape[0], LANE), 1) - 3 * mine[...]
    high = value.astype(BF16).astype(F32)
    middle = (value - high).astype(BF16).astype(F32)
    low = value - high - middle
    return jnp.where(
        lane == 0, high, jnp.where(lane == 1, middle, jnp.where(lane == 2, low, 0.0))
    ).astype(BF16)


def first_kernel(
    chunks, quarter_tiles,
    few, ents, pars, sorted_bus, load, tiles, place, generation, charging, mine,
    compact, spill, base, load_sum, state, rows, *rest,
):
    outs, rest = rest[: chunks // 2 - 1], rest[chunks // 2 - 1 :]
    balance, picked, few_held, ents_held, stage, sems, total = rest
    copy = pltpu.make_async_copy(ents, ents_held, sems.at[2])
    copy.start()
    lists = Lists(few, ents, compact, spill, few_held, ents_held, stage, sems)
    hours, gens = generation.shape
    x = jnp.concatenate([generation[...], -charging[...]], axis=1)
    unit = lax.broadcasted_iota(jnp.int32, pars.shape, 1)
    name = lax.broadcasted_iota(jnp.int32, pars.shape, 0)
    own = pars[...]
    low = jnp.broadcast_to(jnp.where(unit[:1] < gens, 0.0, -own[HIGH : HIGH + 1]), own.shape)
    own = jnp.where(name == LOW, low, own)
    own = jnp.where((name == RAMP) & (unit >= gens), 1e30, own)
    left = jnp.concatenate([split(x), split(own)], axis=0)
    ordered = mxu(left, place[...], NN)
    z = joined(ordered[: 3 * hours])
    state[...] = z
    rows[...] = joined(ordered[3 * hours :])
    put_picked(z, picked)
    copy.wait()
    found = ents_held[START, chunks]
    build(ents_held, sorted_bus, load, tiles, compact, spill, base, load_sum, stage, sems.at[1], found)
    lists.ready(chunks)
    start_flows(base, total, quarter_tiles, 1, chunks // 2)
    balance[...] = own_balance(z, load_sum, mine)
    add_flows(lists, picked, total, balance[...], quarter_tiles, 1, chunks // 2, outs)


def lower_kernel(
    chunks, quarter_tiles,
    few, ents, compact, spill, base, picked, balance,
    out, few_held, ents_held, stage, sems, total,
):
    lists = Lists(few, ents, compact, spill, few_held, ents_held, stage, sems)
    start_flows(base, total, quarter_tiles, 0, 1)
    lists.ready(chunks)
    add_flows(lists, picked, total, balance[...], quarter_tiles, 0, 1, [out])


def hours_kernel(state, back, sent):
    z = state[...]
    stores = sent.shape[1]
    own = -joined(mxu(split(z), back[:, z.shape[1] - stores :], NN))
    send_hours(z, own, sent)


def price_kernel(
    chunks, quarter_tiles, first, last, fresh,
    few, ents, compact, spill, *rest,
):
    bars, rest = rest[: last - first], rest[last - first :]
    if not fresh:
        before, rest = rest[0], rest[1:]
    total, few_held, ents_held, stage, sems, lines = rest
    lists = Lists(few, ents, compact, spill, few_held, ents_held, stage, sems)
    total[...] = jnp.zeros_like(total) if fresh else before[...]
    start_prices(bars, lines, quarter_tiles)
    lists.ready(chunks)
    add_prices(lists, lines, total, quarter_tiles, first, last)


def step_kernel(
    chunks, quarter_tiles, balance_step, final,
    few, ents, compact, spill, before, state, fixed, balance_dual, balances, rows, base, load_sum,
    back, mine, *rest,
):
    start = 2
    bars, rest = rest[: chunks - start], rest[chunks - start :]
    if final:
        next_g, next_p, few_held, ents_held, stage, sems, lines, prices = rest
    else:
        next_state, next_balance, *rest = rest
        outs, rest = rest[: chunks // 2 - 1], rest[chunks // 2 - 1 :]
        balance, picked, few_held, ents_held, stage, sems, lines, prices, total = rest
    lists = Lists(few, ents, compact, spill, few_held, ents_held, stage, sems)
    prices[...] = before[...]
    start_prices(bars, lines, quarter_tiles)
    if not final:
        start_flows(base, total, quarter_tiles, 1, chunks // 2)
    lists.ready(chunks)
    add_prices(lists, lines, prices, quarter_tiles, start, chunks)
    blocks = prices.shape[0] - 1
    price = jnp.concatenate([prices[m] for m in range(blocks)], axis=1)
    old = balance_dual[...]
    new = old + balance_step * jnp.sum(balances[...], axis=1, keepdims=True)
    bb = 2.0 * new - old
    high = rows[HIGH : HIGH + 1]
    z = state[...] - TAU * (bb + price + fixed[...])
    z = jnp.minimum(jnp.maximum(z, rows[LOW : LOW + 1]), high)
    if final:
        gens = next_g.shape[1]
        x = joined(mxu(split(z), back[...], NN))
        next_g[...] = x[:, :gens]
        next_p[...] = -x[:, gens:]
    else:
        next_state[...] = z
        next_balance[...] = new
        put_picked(z, picked)
        balance[...] = own_balance(z, load_sum, mine)
        add_flows(lists, picked, total, balance[...], quarter_tiles, 1, chunks // 2, outs)


def hourly_kernel(
    years, hours, order, final,
    where, state, rows, pars, place, ramp_dual, state_dual,
    *rest,
):
    heard, rest = rest[:years], rest[years:]
    if final:
        fixed, everyone, wide, local, bars, adjoint = rest
    else:
        fixed, ramp_out, state_out, everyone, wide, local, bars, adjoint = rest
    gens = state.shape[1]
    units = adjoint.shape[1]
    cost, ramp_limit = rows[COST : COST + 1], rows[RAMP : RAMP + 1]
    cap = pars[CAP : CAP + 1, gens - units :]
    keep = jnp.log1p(-pars[LOSS : LOSS + 1, gens - units :])
    each = -(-gens // units)
    me = where[0]
    before = lax.rem(me + years - 1, years)
    after = lax.rem(me + 1, years)
    for j in range(years):
        everyone[me ^ order[j]] = heard[j][...]
    wide[8 : 8 + hours] = state[...]
    for j in range(each):
        span = min(units, gens - j * units)
        to = slice(j * units, j * units + span)
        at = hours + each + j
        wide[7:8, to] = everyone[before, at : at + 1, :span]
        at = hours + j
        wide[8 + hours : 9 + hours, to] = everyone[after, at : at + 1, :span]
    ramps = wide[8 : 16 + hours] - wide[7 : 15 + hours]
    old = ramp_dual[...]
    shift = old + SIGMA * ramps
    limit = SIGMA * ramp_limit
    new = shift - jnp.minimum(jnp.maximum(shift, -limit), limit)
    if not final:
        ramp_out[...] = new
    wide[0 : 8 + hours] = 2.0 * new - old
    fixed[...] = cost + wide[0:hours] - wide[1 : 1 + hours]

    step = lax.broadcasted_iota(jnp.int32, (8, units), 0)
    rise = jnp.exp((step + 1).astype(F32) * keep)
    fall = jnp.exp((8 - step).astype(F32) * keep)
    one, two, four, eight = (jnp.exp(k * keep) for k in (1.0, 2.0, 4.0, 8.0))
    closing = 1.0 / (1.0 - jnp.exp(float(years * hours) * keep))
    count = years * hours // 8
    per = hours // 8

    def within(n, _):
        y = everyone[n // per, pl.ds(pl.multiple_of((n % per) * 8, 8), 8), :]
        for by, factor in ((1, one), (2, two), (4, four)):
            y = y + jnp.where(step >= by, factor * pltpu.roll(y, by, 0), 0.0)
        local[n] = y
        return 0

    lax.fori_loop(0, count, within, 0, unroll=8)
    zero = jnp.zeros((1, units), F32)
    finish = lax.fori_loop(0, count, lambda n, c: local[n][7:8] + eight * c, zero, unroll=8)

    def forward(n, c):
        y = local[n]
        state = y + rise * c
        old = state_dual[n]
        shift = old + SIGMA * state
        new = shift - jnp.minimum(jnp.maximum(shift, 0.0), SIGMA * cap)
        if not final:
            state_out[n] = new
        bar = 2.0 * new - old
        for by, factor in ((1, one), (2, two), (4, four)):
            bar = bar + jnp.where(step < 8 - by, factor * pltpu.roll(bar, 8 - by, 0), 0.0)
        bars[n] = bar
        return y[7:8] + eight * c

    lax.fori_loop(0, count, forward, finish * closing, unroll=8)

    def back(i, c):
        return bars[count - 1 - i][0:1] + eight * c

    finish = lax.fori_loop(0, count, back, zero, unroll=8)
    c = lax.fori_loop(0, count - (me + 1) * per, back, finish * closing)
    for j in reversed(range(per)):
        y = bars[me * per + j]
        adjoint[8 * j : 8 * j + 8] = y + fall * c
        c = y[0:1] + eight * c
    fixed[...] -= joined(mxu(split(adjoint[...]), place[gens - units :], NN))


def shards(
    gen_start, charge_start, load, ptdf_tiles, tile_row, tile_col, gen_bus, stor_bus,
    gen_cost, gen_max, ramp_limit, stor_power, stor_loss, stor_cap, flow_limit,
):
    hours, gens = gen_start.shape
    stores = charge_start.shape[1]
    units = gens + stores
    kt = ptdf_tiles.shape[0]
    bus_tiles = load.shape[1] // LANE
    chunks = lax.axis_size("bus")
    years = lax.axis_size("tm")
    lines = flow_limit.shape[0] // chunks
    quarter_tiles = lines // LANE
    blocks = units // LANE
    line_tiles = chunks * quarter_tiles
    mine = lax.axis_index("bus")
    balance_step = SIGMA / (gens * chunks)
    cap = blocks * kt + LARGE
    kept = min(cap, KEPT) // SMALL * SMALL
    sent_rows = -(-(hours + 2 * -(-units // stores)) // 8) * 8
    groups = years * hours // 8

    def like(*shape, dtype=F32):
        return jax.ShapeDtypeStruct(shape, dtype)

    def placed(count, *parts):
        total = 0
        for row, at, x in parts:
            before = row * units + at
            total += jnp.pad(x, (before, count * units - before - x.shape[0]))
        return total.reshape(count, units)

    pars = placed(
        8,
        (COST, 0, gen_cost),
        (HIGH, 0, gen_max),
        (HIGH, gens, stor_power),
        (RAMP, 0, ramp_limit),
        (CAP, gens, stor_cap),
        (LOSS, gens, stor_loss),
    )
    whole = placed(
        2, (BUS, 0, gen_bus), (BUS, gens, stor_bus), (TILES, 0, tile_row), (TILES, LANE, tile_col)
    )

    width = -(-(cap + SMALL) // LANE) * LANE
    where = lax.axis_index("tm").astype(jnp.int32).reshape(1)
    near_line = mine.astype(jnp.uint32) * lines
    far_line = (mine ^ (chunks // 2)).astype(jnp.uint32) * lines
    whole, where, near_line, far_line = lax.optimization_barrier(
        (whole, where, near_line, far_line)
    )
    mine_row = jnp.broadcast_to(mine.astype(jnp.int32), (1, LANE))
    place, back, sorted_bus, ents, few = pl.pallas_call(
        functools.partial(plan_kernel, chunks, quarter_tiles, kt),
        out_shape=(
            like(units, units, dtype=BF16),
            like(units, units, dtype=BF16),
            like(blocks, LANE, LANE),
            like(8, width, dtype=jnp.int32),
            like(4, FEW, dtype=jnp.int32),
        ),
        in_specs=[vmem()] * 2,
        out_specs=(vmem(),) * 5,
        compiler_params=params(STEP_MIB),
        name="plan",
        cost_estimate=cost(3, 3 * 10**9),
    )(mine_row, whole)

    pair_out = (like(hours, 2 * lines + LANE, dtype=BF16),)
    step_out = pair_out * (chunks // 2 - 1)
    step_out += (like(hours, LANE, dtype=BF16), like(blocks + 1, hours, LANE, dtype=BF16))
    staging = [
        pltpu.SMEM((4, FEW), jnp.int32),
        pltpu.SMEM((8, width), jnp.int32),
        pltpu.VMEM((LANE, LANE), BF16),
        pltpu.SemaphoreType.DMA((3,)),
    ]
    lists = [vmem(), vmem(), vmem(), hbm()]

    def flow_scratch(pairs):
        return [pltpu.VMEM((hours, (2 * pairs * quarter_tiles + 1) * LANE), F32)]

    def line_scratch(count):
        return pltpu.VMEM((hours, (count * quarter_tiles + 1) * LANE), BF16)

    price_shape = (blocks + 1, hours, LANE)
    first_call = pl.pallas_call(
        functools.partial(first_kernel, chunks, quarter_tiles),
        out_shape=(
            like(kept + SMALL, LANE, LANE, dtype=BF16),
            like(max(cap - kept, SPILL), LANE, LANE, dtype=BF16),
            like(hours, (line_tiles + 1) * LANE),
            like(hours, 1),
            like(hours, units),
            like(8, units),
        )
        + step_out,
        in_specs=[vmem()] * 10,
        out_specs=(vmem(), hbm()) + (vmem(),) * (len(step_out) + 4),
        scratch_shapes=staging + flow_scratch(chunks // 2 - 1),
        compiler_params=params(STEP_MIB),
        name="first",
        cost_estimate=cost(9),
    )

    lower_call = pl.pallas_call(
        functools.partial(lower_kernel, chunks, quarter_tiles),
        out_shape=pair_out[0],
        in_specs=lists + [vmem()] * 3,
        out_specs=vmem(),
        scratch_shapes=staging + flow_scratch(1),
        compiler_params=params(STEP_MIB),
        name="lower",
        cost_estimate=cost(2),
    )
    hours_call = pl.pallas_call(
        hours_kernel,
        out_shape=like(sent_rows, stores),
        in_specs=[vmem()] * 2,
        out_specs=vmem(),
        compiler_params=params(STEP_MIB),
        name="hours",
        cost_estimate=cost(1),
    )

    def price_call(first, last, fresh):
        return pl.pallas_call(
            functools.partial(price_kernel, chunks, quarter_tiles, first, last, fresh),
            out_shape=like(*price_shape),
            in_specs=lists + [vmem()] * (last - first + (not fresh)),
            out_specs=vmem(),
            scratch_shapes=staging + [line_scratch(last - first)],
            compiler_params=params(STEP_MIB),
            name="price",
            cost_estimate=cost(2),
        )

    tail = 2

    def step_call(final):
        scratch = staging + [line_scratch(chunks - tail), pltpu.VMEM(price_shape, F32)]
        if final:
            shape = (like(hours, gens), like(hours, stores))
        else:
            shape = (like(hours, units), like(hours, 1)) + step_out
            scratch += flow_scratch(chunks // 2 - 1)
        return pl.pallas_call(
            functools.partial(step_kernel, chunks, quarter_tiles, balance_step, final),
            out_shape=shape,
            in_specs=lists + [vmem()] * (10 + chunks - tail),
            out_specs=(vmem(),) * len(shape),
            scratch_shapes=scratch,
            compiler_params=params(STEP_MIB),
            name="step",
            cost_estimate=cost(4),
        )

    spans = [1 << b for b in reversed(range(years.bit_length() - 1))]
    order = [0]
    for bit in spans:
        order += [j ^ bit for j in order]

    def hourly_call(final):
        shape = (like(hours, units),)
        if not final:
            shape += (like(hours + 8, units), like(groups, 8, stores))
        return pl.pallas_call(
            functools.partial(hourly_kernel, years, hours, order, final),
            out_shape=shape,
            in_specs=[smem()] + [vmem()] * (6 + years),
            out_specs=(vmem(),) * len(shape),
            scratch_shapes=[
                pltpu.VMEM((years, sent_rows, stores), F32),
                pltpu.VMEM((hours + 16, units), F32),
                pltpu.VMEM((groups, 8, stores), F32),
                pltpu.VMEM((groups, 8, stores), F32),
                pltpu.VMEM((hours, stores), F32),
            ],
            compiler_params=params(STEP_MIB),
            name="hourly",
            cost_estimate=cost(2.4),
        )

    def swap(x, bit, axis="bus"):
        size = lax.axis_size(axis)
        return lax.ppermute(x, axis, [(i, i ^ bit) for i in range(size)])

    def hear(stacked, over):
        for bit in over:
            stacked = jnp.concatenate([stacked, swap(stacked, bit, "tm")])
        return stacked

    bits = [1 << b for b in range(chunks.bit_length() - 1)]
    near_dual = jnp.zeros((hours, lines), F32)
    far_dual = jnp.zeros((hours, lines), F32)
    ramp_dual = jnp.zeros((hours + 8, units), F32)
    state_dual = jnp.zeros((groups, 8, stores), F32)
    balance_dual = jnp.zeros((hours, 1), F32)
    compact, spill, base, load_sum, state, unit_rows, *made = first_call(
        few, ents, pars, sorted_bus, load, ptdf_tiles, place, gen_start, charge_start, mine_row
    )
    held = (few, ents, compact, spill)
    half_way = chunks // 2

    def renew(dual, flows, from_line):
        limits = SIGMA * lax.dynamic_slice(flow_limit, (from_line,), (lines,))
        shift = dual + SIGMA * flows
        after = shift - jnp.clip(shift, -limits, limits)
        return after, (2.0 * after - dual).astype(BF16)

    for iteration in range(ITERS):
        final = iteration == ITERS - 1
        *made, balance, picked = made
        made = [lower_call(*held, base, picked, balance), *made]
        sums = [x.astype(F32) for x in made]
        for bit in bits[:-1]:
            for d in range(half_way):
                if d & bit and not d & (bit - 1):
                    sums[d ^ bit] = sums[d ^ bit] + swap(sums[d].astype(BF16), bit).astype(F32)
        ready = sums[0].astype(BF16)
        got = swap(ready, half_way)
        state, ready = lax.optimization_barrier((state, ready))
        heard = hear(hours_call(state, back)[None], spans)
        fixed, *duals = hourly_call(final)(
            where, state, unit_rows, pars, place, ramp_dual, state_dual,
            *[heard[j] for j in range(years)],
        )
        got, fixed = lax.optimization_barrier((got, fixed))
        ours, theirs = ready.astype(F32), got.astype(F32)
        balances = ours[:, lines : lines + LANE] + theirs[:, lines : lines + LANE]
        near_dual, near = renew(
            near_dual, ours[:, :lines] + theirs[:, lines + LANE :], near_line
        )
        far_dual, far = renew(far_dual, ours[:, lines + LANE :] + theirs[:, :lines], far_line)
        have = {0: (near, far)}
        for bit in reversed(bits[:-1]):
            for d in list(have):
                have[d | bit] = tuple(swap(x, bit) for x in have[d])
        bars = [x for d in range(half_way) for x in have[d]]
        prices = price_call(0, tail, True)(*held, *bars[:tail])
        made = step_call(final)(
            *held, prices, state, fixed, balance_dual, balances, unit_rows, base, load_sum, back,
            mine_row, *bars[tail:],
        )
        if not final:
            ramp_dual, state_dual = duals
            state, balance_dual, *made = made
    return *made, near_dual


STEP_MIB = 16
SPILL = 1500


def solution(mesh):
    rows = P(("scen", "tm"), "bus")
    return jax.shard_map(
        shards,
        mesh=mesh,
        in_specs=(rows, rows, rows, P("bus", None, None)) + (P("bus"),) * 10 + (P(),),
        out_specs=(rows, rows, rows),
        check_vma=False,
    )
```

```python
import functools

import jax
import jax.numpy as jnp
from jax import lax
from jax.experimental import pallas as pl
from jax.experimental.pallas import tpu as pltpu
from jax.sharding import PartitionSpec as P

ITERS = 3
TAU = 0.5
SIGMA = 0.5
LANE = 128
GROUPS = (64, 32, 8)
LARGE, SMALL = GROUPS[0], GROUPS[-1]
KEPT = 160
F32 = jnp.float32
BF16 = jnp.bfloat16

NN = (((1,), (0,)), ((), ()))
NT = (((1,), (1,)), ((), ()))


def mxu(a, b, dims):
    return lax.dot_general(a, b, dims, preferred_element_type=F32)


def smem():
    return pl.BlockSpec(memory_space=pltpu.SMEM)


def vmem():
    return pl.BlockSpec(memory_space=pltpu.VMEM)


def hbm():
    return pl.BlockSpec(memory_space=pl.ANY)


def params(mib):
    return pltpu.CompilerParams(vmem_limit_bytes=mib * 1024 * 1024)


def cost(us, flops=0):
    return pl.CostEstimate(flops=flops, bytes_accessed=int(us * 3.0e6), transcendentals=0)


def lanes(at):
    return pl.ds(pl.multiple_of(at * LANE, LANE), LANE)


ROW, BLOCK, START, TILE, COLUMN, FIRST = range(6)
FEW = 256
LOW = 7

COST, HIGH, RAMP, CAP, LOSS, BUS, TILES = range(7)


def plan_kernel(
    chunks, quarter_tiles, kt,
    mine, pars,
    place, back, sorted_bus, ents, few,
):
    units = place.shape[0]
    blocks = units // LANE
    square = (LANE, LANE)
    sub = lax.broadcasted_iota(jnp.int32, square, 0).astype(F32)
    lane = lax.broadcasted_iota(jnp.int32, square, 1).astype(F32)
    eye = sub == lane

    def column(row):
        return jnp.sum(jnp.where(eye, jnp.broadcast_to(row, square), 0.0), axis=1, keepdims=True)

    def over_sub(mask, values):
        return jnp.sum(jnp.where(mask, values, 0.0), axis=0, keepdims=True)

    def over_lane(mask, values):
        return jnp.sum(jnp.where(mask, values, 0.0), axis=1, keepdims=True)

    bus = pars[BUS : BUS + 1]
    unit = lax.broadcasted_iota(jnp.int32, (1, units), 1).astype(F32)
    key = bus * units + unit
    ordered = jnp.zeros((1, units), F32)
    starts = jnp.zeros((1, LANE), F32)
    stops = jnp.zeros((1, LANE), F32)
    ranks = []
    for b in range(blocks):
        here = column(bus[:, b * LANE : (b + 1) * LANE])
        rank = over_lane(key < here * units + (sub[:, :1] + float(b * LANE)), 1.0)
        mine_at = rank == unit
        place[b * LANE : (b + 1) * LANE] = jnp.where(mine_at, 1.0, 0.0).astype(BF16)
        ordered += over_sub(mine_at, here)
        ranks.append(over_sub(eye, rank))
        starts += over_sub(here < lane * LANE, 1.0)
        stops += over_sub(here < (lane + 1.0) * LANE, 1.0)
    ranks = jnp.concatenate(ranks, axis=1)
    for b in range(blocks):
        back[b * LANE : (b + 1) * LANE] = jnp.where(
            sub[:, :1] + float(b * LANE) == ranks, 1.0, 0.0
        ).astype(BF16)
        sorted_bus[b] = jnp.broadcast_to(column(ordered[:, b * LANE : (b + 1) * LANE]), square)

    row = pars[TILES : TILES + 1, :LANE].astype(jnp.int32)
    col = pars[TILES : TILES + 1, LANE : 2 * LANE]
    chunk = jnp.zeros_like(row)
    for d in range(1, chunks):
        chunk = chunk + (row >= d * quarter_tiles).astype(jnp.int32)
    relative = chunk ^ mine[...]
    half = chunks // 2
    slot = 2 * (relative & (half - 1)) + (relative >= half).astype(jnp.int32)
    relative = ((slot - chunk) * quarter_tiles + row).astype(F32)
    number = lane[:1]
    tile_key = jnp.where(number < kt, relative, float(chunks * quarter_tiles)) * LANE + number
    rank = over_sub(column(tile_key) < tile_key, 1.0)
    sorting = rank == sub
    relative, col, tile = (over_lane(sorting, x) for x in (relative, col, number))
    first, last = over_lane(lane == col, starts), over_lane(lane == col, stops)
    block = jnp.minimum(jnp.floor(first * (1.0 / LANE)), float(blocks - 1))
    until = jnp.floor((last - 1.0) * (1.0 / LANE))
    count = jnp.where(last > first, until - block + 1.0, 1.0)
    count = jnp.where(sub[:, :1] < kt, count, 0.0)
    at = over_lane(lane < sub, over_sub(eye, count))
    entry = lax.broadcasted_iota(jnp.int32, (1, ents.shape[1]), 1).astype(F32)
    inside = (at <= entry) & (entry < at + count)
    ents[...] = jnp.zeros_like(ents)
    for name, values in (
        (ROW, relative),
        (BLOCK, block - at + entry),
        (TILE, tile),
        (COLUMN, col),
        (FIRST, (entry == at).astype(F32)),
    ):
        ents[name : name + 1] = over_sub(inside, values).astype(jnp.int32)
    ents[START : START + 1, :LANE] = over_sub(relative < lane * quarter_tiles, count).astype(
        jnp.int32
    )
    few[...] = ents[: few.shape[0], :FEW]


def sweep(lo, hi, body):
    hi = jnp.maximum(lo, hi)
    for size in GROUPS[:-1]:

        def group(n, _, size=size, lo=lo):
            for u in range(size):
                body(lo + n * size + u, None)
            return 0

        count = (hi - lo) // size
        lax.fori_loop(0, count, group, 0)
        lo = lo + count * size

    def short(n, _):
        for u in range(SMALL):
            e = lo + n * SMALL + u
            body(e, e < hi)
        return 0

    lax.fori_loop(0, (hi - lo + SMALL - 1) // SMALL, short, 0)


class Lists:
    def __init__(self, few, ents, compact, spill, few_held, ents_held, stage, sems):
        self.ents, self.compact, self.spill = ents, compact, spill
        self.few_held, self.ents_held, self.stage, self.sems = few_held, ents_held, stage, sems
        self.copy = pltpu.make_async_copy(few, few_held, sems.at[0])
        self.copy.start()
        self.kept = compact.shape[0] - SMALL

    def ready(self, chunks):
        self.copy.wait()

        @pl.when(self.few_held[START, chunks] > self.kept)
        def _():
            copy = pltpu.make_async_copy(self.ents, self.ents_held, self.sems.at[1])
            copy.start()
            copy.wait()

    def sweep(self, first, last, body, matrices=None):
        matrices = self.compact if matrices is None else matrices
        lo, hi = self.few_held[START, first], self.few_held[START, last]
        held, more = self.few_held, self.ents_held
        sweep(
            lo,
            jnp.minimum(hi, self.kept),
            lambda e, live: body(held[ROW, e], held[BLOCK, e], live, matrices.at[e], True),
        )

        def fetched(e, _):
            copy = pltpu.make_async_copy(self.spill.at[e - self.kept], self.stage, self.sems.at[1])
            copy.start()
            copy.wait()
            body(more[ROW, e], more[BLOCK, e], None, self.stage, False)
            return 0

        lax.fori_loop(jnp.maximum(lo, self.kept), hi, fetched, 0)


def split(x):
    high = x.astype(BF16)
    rest = x - high.astype(F32)
    middle = rest.astype(BF16)
    low = (rest - middle.astype(F32)).astype(BF16)
    return jnp.concatenate([high, middle, low], axis=0)


def joined(x):
    rows = x.shape[0] // 3
    return x[:rows] + x[rows : 2 * rows] + x[2 * rows :]


def pick(live, value, other):
    return value if live is None else jnp.where(live, value, other)


def build(ents, sorted_bus, load, tiles, compact, spill, base, load_sum, stage, sem, found):
    kept = compact.shape[0] - SMALL
    hours = load.shape[0]
    spare = base.shape[1] // LANE - 1
    base[...] = jnp.zeros_like(base)
    lane = lax.broadcasted_iota(jnp.int32, (LANE, LANE), 1)

    def restricted(e, live):
        col = pick(live, ents[COLUMN, e], 0)
        row = jnp.where(pick(live, ents[FIRST, e], 0) == 1, ents[ROW, e], spare)
        bus = sorted_bus[pick(live, ents[BLOCK, e], 0)]
        hot = jnp.where(bus == (lane + col * LANE).astype(F32), 1.0, 0.0).astype(BF16)
        left = jnp.concatenate([load[:, lanes(col)], hot], axis=0)
        both = mxu(left, tiles[pick(live, ents[TILE, e], 0)], NT)
        base[:, lanes(row)] -= both[:hours]
        return both[hours:].astype(BF16)

    def keep(e, live):
        compact[e] = restricted(e, live)

    def put_out(e, _):
        stage[...] = restricted(e, None)
        copy = pltpu.make_async_copy(stage, spill.at[e - kept], sem)
        copy.start()
        copy.wait()
        return 0

    sweep(jnp.int32(0), jnp.minimum(found, kept), keep)
    lax.fori_loop(jnp.int32(kept), found, put_out, 0)
    total = load[:, :LANE].astype(F32)
    for c in range(1, load.shape[1] // LANE):
        total += load[:, c * LANE : (c + 1) * LANE].astype(F32)
    load_sum[...] = jnp.sum(total, axis=1, keepdims=True)


def start_flows(base, total, quarter_tiles, first, last):
    width = 2 * quarter_tiles * LANE
    total[:, : (last - first) * width] = base[:, first * width : last * width]


def add_flows(lists, picked, total, balance, quarter_tiles, first, last, outs):
    width = quarter_tiles * LANE
    origin, spare = 2 * first * quarter_tiles, 2 * (last - first) * quarter_tiles
    blocks = picked.shape[0] - 1

    def entry(row, m, live, matrix, kept):
        row, m = pick(live, row - origin, spare), pick(live, m, blocks)
        total[:, lanes(row)] += mxu(picked[m], matrix[...], NN)

    lists.sweep(2 * first, 2 * last, entry)
    for d, out in enumerate(outs):
        at = 2 * d * width
        out[:, :width] = total[:, at : at + width].astype(BF16)
        out[:, width : width + LANE] = balance
        out[:, width + LANE :] = total[:, at + width : at + 2 * width].astype(BF16)


def start_prices(bars, lines, quarter_tiles):
    width = 2 * quarter_tiles * LANE
    for d, bar in enumerate(bars):
        lines[:, d * width : (d + 1) * width] = bar[...]


def add_prices(lists, turned, lines, total, quarter_tiles, first, last):
    origin = first * quarter_tiles
    spare, blocks = (last - first) * quarter_tiles, total.shape[0] - 1

    def entry(row, m, live, matrix, kept):
        row, m = pick(live, row - origin, spare), pick(live, m, blocks)
        total[m] += mxu(lines[:, lanes(row)], matrix[...], NN if kept else NT)

    lists.sweep(first, last, entry, turned)


def put_picked(z, picked):
    for m in range(picked.shape[0] - 1):
        picked[m] = z[:, m * LANE : (m + 1) * LANE].astype(BF16)


def send_hours(z, own, sent):
    hours, units = z.shape
    stores = own.shape[1]
    sent[:hours] = own
    sent[hours:] = jnp.zeros_like(sent[hours:])
    each = -(-units // stores)
    for i, row in enumerate((z[:1], z[hours - 1 :])):
        for j in range(each):
            piece = row[:, j * stores : min((j + 1) * stores, units)]
            sent[hours + i * each + j : hours + i * each + j + 1, : piece.shape[1]] = piece


def own_balance(z, load_sum, mine):
    value = jnp.sum(z, axis=1, keepdims=True) - load_sum[...]
    lane = lax.broadcasted_iota(jnp.int32, (z.shape[0], LANE), 1) - 3 * mine[...]
    high = value.astype(BF16).astype(F32)
    middle = (value - high).astype(BF16).astype(F32)
    low = value - high - middle
    return jnp.where(
        lane == 0, high, jnp.where(lane == 1, middle, jnp.where(lane == 2, low, 0.0))
    ).astype(BF16)


def first_kernel(
    chunks, quarter_tiles,
    few, ents, pars, sorted_bus, load, tiles, place, generation, charging, mine,
    compact, spill, base, load_sum, state, rows, *rest,
):
    outs, rest = rest[: chunks // 2 - 1], rest[chunks // 2 - 1 :]
    balance, picked, few_held, ents_held, stage, sems, total = rest
    copy = pltpu.make_async_copy(ents, ents_held, sems.at[2])
    copy.start()
    lists = Lists(few, ents, compact, spill, few_held, ents_held, stage, sems)
    hours, gens = generation.shape
    x = jnp.concatenate([generation[...], -charging[...]], axis=1)
    unit = lax.broadcasted_iota(jnp.int32, pars.shape, 1)
    name = lax.broadcasted_iota(jnp.int32, pars.shape, 0)
    own = pars[...]
    low = jnp.broadcast_to(jnp.where(unit[:1] < gens, 0.0, -own[HIGH : HIGH + 1]), own.shape)
    own = jnp.where(name == LOW, low, own)
    own = jnp.where((name == RAMP) & (unit >= gens), 1e30, own)
    left = jnp.concatenate([split(x), split(own)], axis=0)
    ordered = mxu(left, place[...], NN)
    z = joined(ordered[: 3 * hours])
    state[...] = z
    rows[...] = joined(ordered[3 * hours :])
    put_picked(z, picked)
    copy.wait()
    found = ents_held[START, chunks]
    build(ents_held, sorted_bus, load, tiles, compact, spill, base, load_sum, stage, sems.at[1], found)
    lists.ready(chunks)
    start_flows(base, total, quarter_tiles, 1, chunks // 2)
    balance[...] = own_balance(z, load_sum, mine)
    add_flows(lists, picked, total, balance[...], quarter_tiles, 1, chunks // 2, outs)


def lower_kernel(
    chunks, quarter_tiles,
    few, ents, compact, spill, base, picked, balance,
    out, few_held, ents_held, stage, sems, total,
):
    lists = Lists(few, ents, compact, spill, few_held, ents_held, stage, sems)
    start_flows(base, total, quarter_tiles, 0, 1)
    lists.ready(chunks)
    add_flows(lists, picked, total, balance[...], quarter_tiles, 0, 1, [out])


def hours_kernel(state, back, sent):
    z = state[...]
    stores = sent.shape[1]
    own = -joined(mxu(split(z), back[:, z.shape[1] - stores :], NN))
    send_hours(z, own, sent)


def turn_kernel(chunks, few, compact, turned, few_held, sem):
    copy = pltpu.make_async_copy(few, few_held, sem)
    copy.start()
    square = (LANE, LANE)
    eye = lax.broadcasted_iota(jnp.int32, square, 0) == lax.broadcasted_iota(jnp.int32, square, 1)
    eye = jnp.where(eye, 1.0, 0.0).astype(BF16)
    copy.wait()

    def entry(e, live):
        turned[e] = mxu(eye, compact[e], NT).astype(BF16)

    sweep(jnp.int32(0), jnp.minimum(few_held[START, chunks], compact.shape[0] - SMALL), entry)


def price_kernel(
    chunks, quarter_tiles, first, last, fresh,
    few, ents, compact, spill, turned, *rest,
):
    count = (last - first) // 2
    bars, rest = rest[:count], rest[count:]
    if not fresh:
        before, rest = rest[0], rest[1:]
    total, few_held, ents_held, stage, sems, lines = rest
    lists = Lists(few, ents, compact, spill, few_held, ents_held, stage, sems)
    total[...] = jnp.zeros_like(total) if fresh else before[...]
    start_prices(bars, lines, quarter_tiles)
    lists.ready(chunks)
    add_prices(lists, turned, lines, total, quarter_tiles, first, last)


def step_kernel(
    chunks, quarter_tiles, balance_step, final,
    few, ents, compact, spill, turned, before, state, fixed, balance_dual, balances, rows, base,
    load_sum, back, mine, *rest,
):
    start = 2
    bars, rest = rest[: chunks // 2 - 1], rest[chunks // 2 - 1 :]
    if final:
        dual, next_g, next_p, line_dual, few_held, ents_held, stage, sems, lines, prices = rest
        out = pltpu.make_async_copy(dual, line_dual, sems.at[2])
        out.start()
    else:
        next_state, next_balance, *rest = rest
        outs, rest = rest[: chunks // 2 - 1], rest[chunks // 2 - 1 :]
        balance, picked, few_held, ents_held, stage, sems, lines, prices, total = rest
    lists = Lists(few, ents, compact, spill, few_held, ents_held, stage, sems)
    prices[...] = before[...]
    start_prices(bars, lines, quarter_tiles)
    if not final:
        start_flows(base, total, quarter_tiles, 1, chunks // 2)
    lists.ready(chunks)
    add_prices(lists, turned, lines, prices, quarter_tiles, start, chunks)
    blocks = prices.shape[0] - 1
    price = jnp.concatenate([prices[m] for m in range(blocks)], axis=1)
    old = balance_dual[...]
    new = old + balance_step * jnp.sum(balances[...], axis=1, keepdims=True)
    bb = 2.0 * new - old
    high = rows[HIGH : HIGH + 1]
    z = state[...] - TAU * (bb + price + fixed[...])
    z = jnp.minimum(jnp.maximum(z, rows[LOW : LOW + 1]), high)
    if final:
        gens = next_g.shape[1]
        x = joined(mxu(split(z), back[...], NN))
        next_g[...] = x[:, :gens]
        next_p[...] = -x[:, gens:]
        out.wait()
    else:
        next_state[...] = z
        next_balance[...] = new
        put_picked(z, picked)
        balance[...] = own_balance(z, load_sum, mine)
        add_flows(lists, picked, total, balance[...], quarter_tiles, 1, chunks // 2, outs)


def hourly_kernel(
    years, hours, order, final,
    where, state, rows, pars, place, ramp_dual, state_dual,
    *rest,
):
    heard, rest = rest[:years], rest[years:]
    if final:
        fixed, everyone, wide, local, bars, adjoint = rest
    else:
        fixed, ramp_out, state_out, everyone, wide, local, bars, adjoint = rest
    gens = state.shape[1]
    units = adjoint.shape[1]
    cost, ramp_limit = rows[COST : COST + 1], rows[RAMP : RAMP + 1]
    cap = pars[CAP : CAP + 1, gens - units :]
    keep = jnp.log1p(-pars[LOSS : LOSS + 1, gens - units :])
    each = -(-gens // units)
    me = where[0]
    before = lax.rem(me + years - 1, years)
    after = lax.rem(me + 1, years)
    for j in range(years):
        everyone[me ^ order[j]] = heard[j][...]
    wide[8 : 8 + hours] = state[...]
    for j in range(each):
        span = min(units, gens - j * units)
        to = slice(j * units, j * units + span)
        at = hours + each + j
        wide[7:8, to] = everyone[before, at : at + 1, :span]
        at = hours + j
        wide[8 + hours : 9 + hours, to] = everyone[after, at : at + 1, :span]
    ramps = wide[8 : 16 + hours] - wide[7 : 15 + hours]
    old = ramp_dual[...]
    shift = old + SIGMA * ramps
    limit = SIGMA * ramp_limit
    new = shift - jnp.minimum(jnp.maximum(shift, -limit), limit)
    if not final:
        ramp_out[...] = new
    wide[0 : 8 + hours] = 2.0 * new - old
    fixed[...] = cost + wide[0:hours] - wide[1 : 1 + hours]

    step = lax.broadcasted_iota(jnp.int32, (8, units), 0)
    rise = jnp.exp((step + 1).astype(F32) * keep)
    fall = jnp.exp((8 - step).astype(F32) * keep)
    one, two, four, eight = (jnp.exp(k * keep) for k in (1.0, 2.0, 4.0, 8.0))
    closing = 1.0 / (1.0 - jnp.exp(float(years * hours) * keep))
    count = years * hours // 8
    per = hours // 8

    def within(n, _):
        y = everyone[n // per, pl.ds(pl.multiple_of((n % per) * 8, 8), 8), :]
        for by, factor in ((1, one), (2, two), (4, four)):
            y = y + jnp.where(step >= by, factor * pltpu.roll(y, by, 0), 0.0)
        local[n] = y
        return 0

    lax.fori_loop(0, count, within, 0, unroll=8)
    zero = jnp.zeros((1, units), F32)
    finish = lax.fori_loop(0, count, lambda n, c: local[n][7:8] + eight * c, zero, unroll=8)

    def forward(n, c):
        y = local[n]
        state = y + rise * c
        old = state_dual[n]
        shift = old + SIGMA * state
        new = shift - jnp.minimum(jnp.maximum(shift, 0.0), SIGMA * cap)
        if not final:
            state_out[n] = new
        bar = 2.0 * new - old
        for by, factor in ((1, one), (2, two), (4, four)):
            bar = bar + jnp.where(step < 8 - by, factor * pltpu.roll(bar, 8 - by, 0), 0.0)
        bars[n] = bar
        return y[7:8] + eight * c

    lax.fori_loop(0, count, forward, finish * closing, unroll=8)

    def back(i, c):
        return bars[count - 1 - i][0:1] + eight * c

    finish = lax.fori_loop(0, count, back, zero, unroll=8)
    c = lax.fori_loop(0, count - (me + 1) * per, back, finish * closing)
    for j in reversed(range(per)):
        y = bars[me * per + j]
        adjoint[8 * j : 8 * j + 8] = y + fall * c
        c = y[0:1] + eight * c
    fixed[...] -= joined(mxu(split(adjoint[...]), place[gens - units :], NN))


def shards(
    gen_start, charge_start, load, ptdf_tiles, tile_row, tile_col, gen_bus, stor_bus,
    gen_cost, gen_max, ramp_limit, stor_power, stor_loss, stor_cap, flow_limit,
):
    hours, gens = gen_start.shape
    stores = charge_start.shape[1]
    units = gens + stores
    kt = ptdf_tiles.shape[0]
    bus_tiles = load.shape[1] // LANE
    chunks = lax.axis_size("bus")
    years = lax.axis_size("tm")
    lines = flow_limit.shape[0] // chunks
    quarter_tiles = lines // LANE
    blocks = units // LANE
    line_tiles = chunks * quarter_tiles
    mine = lax.axis_index("bus")
    balance_step = SIGMA / (gens * chunks)
    cap = blocks * kt + LARGE
    kept = min(cap, KEPT) // SMALL * SMALL
    sent_rows = -(-(hours + 2 * -(-units // stores)) // 8) * 8
    groups = years * hours // 8

    def like(*shape, dtype=F32):
        return jax.ShapeDtypeStruct(shape, dtype)

    def placed(*parts):
        total = 0
        for row, at, x in parts:
            before = row * units + at
            total += jnp.pad(x, (before, 8 * units - before - x.shape[0]))
        return total

    pars = placed(
        (COST, 0, gen_cost),
        (HIGH, 0, gen_max),
        (HIGH, gens, stor_power),
        (RAMP, 0, ramp_limit),
        (CAP, gens, stor_cap),
        (LOSS, gens, stor_loss),
    ) + placed(
        (BUS, 0, gen_bus), (BUS, gens, stor_bus), (TILES, 0, tile_row), (TILES, LANE, tile_col)
    ).astype(F32)
    pars = pars.reshape(8, units)

    width = -(-(cap + SMALL) // LANE) * LANE
    where = lax.axis_index("tm").astype(jnp.int32).reshape(1)
    near_line = mine.astype(jnp.uint32) * lines
    far_line = (mine ^ (chunks // 2)).astype(jnp.uint32) * lines
    pars, where, near_line, far_line = lax.optimization_barrier(
        (pars, where, near_line, far_line)
    )
    mine_row = jnp.broadcast_to(mine.astype(jnp.int32), (1, LANE))
    place, back, sorted_bus, ents, few = pl.pallas_call(
        functools.partial(plan_kernel, chunks, quarter_tiles, kt),
        out_shape=(
            like(units, units, dtype=BF16),
            like(units, units, dtype=BF16),
            like(blocks, LANE, LANE),
            like(8, width, dtype=jnp.int32),
            like(4, FEW, dtype=jnp.int32),
        ),
        in_specs=[vmem()] * 2,
        out_specs=(vmem(),) * 5,
        compiler_params=params(STEP_MIB),
        name="plan",
        cost_estimate=cost(3, 3 * 10**9),
    )(mine_row, pars)

    pair_out = (like(hours, 2 * lines + LANE, dtype=BF16),)
    step_out = pair_out * (chunks // 2 - 1)
    step_out += (like(hours, LANE, dtype=BF16), like(blocks + 1, hours, LANE, dtype=BF16))
    staging = [
        pltpu.SMEM((4, FEW), jnp.int32),
        pltpu.SMEM((8, width), jnp.int32),
        pltpu.VMEM((LANE, LANE), BF16),
        pltpu.SemaphoreType.DMA((3,)),
    ]
    lists = [vmem(), vmem(), vmem(), hbm()]

    def flow_scratch(pairs):
        return [pltpu.VMEM((hours, (2 * pairs * quarter_tiles + 1) * LANE), F32)]

    def line_scratch(count):
        return pltpu.VMEM((hours, (count * quarter_tiles + 1) * LANE), BF16)

    price_shape = (blocks + 1, hours, LANE)
    first_call = pl.pallas_call(
        functools.partial(first_kernel, chunks, quarter_tiles),
        out_shape=(
            like(kept + SMALL, LANE, LANE, dtype=BF16),
            like(max(cap - kept, SPILL), LANE, LANE, dtype=BF16),
            like(hours, (line_tiles + 1) * LANE),
            like(hours, 1),
            like(hours, units),
            like(8, units),
        )
        + step_out,
        in_specs=[vmem()] * 10,
        out_specs=(vmem(), hbm()) + (vmem(),) * (len(step_out) + 4),
        scratch_shapes=staging + flow_scratch(chunks // 2 - 1),
        compiler_params=params(STEP_MIB),
        name="first",
        cost_estimate=cost(9),
    )

    turn_call = pl.pallas_call(
        functools.partial(turn_kernel, chunks),
        out_shape=like(kept + SMALL, LANE, LANE, dtype=BF16),
        in_specs=[vmem(), vmem()],
        out_specs=vmem(),
        scratch_shapes=[pltpu.SMEM((4, FEW), jnp.int32), pltpu.SemaphoreType.DMA],
        compiler_params=params(STEP_MIB),
        name="turn",
        cost_estimate=cost(4),
    )
    lower_call = pl.pallas_call(
        functools.partial(lower_kernel, chunks, quarter_tiles),
        out_shape=pair_out[0],
        in_specs=lists + [vmem()] * 3,
        out_specs=vmem(),
        scratch_shapes=staging + flow_scratch(1),
        compiler_params=params(STEP_MIB),
        name="lower",
        cost_estimate=cost(2),
    )
    hours_call = pl.pallas_call(
        hours_kernel,
        out_shape=like(sent_rows, stores),
        in_specs=[vmem()] * 2,
        out_specs=vmem(),
        compiler_params=params(STEP_MIB),
        name="hours",
        cost_estimate=cost(1),
    )

    def price_call(first, last, fresh):
        return pl.pallas_call(
            functools.partial(price_kernel, chunks, quarter_tiles, first, last, fresh),
            out_shape=like(*price_shape),
            in_specs=lists + [vmem()] * (1 + (last - first) // 2 + (not fresh)),
            out_specs=vmem(),
            scratch_shapes=staging + [line_scratch(last - first)],
            compiler_params=params(STEP_MIB),
            name="price",
            cost_estimate=cost(2),
        )

    tail = 2

    def step_call(final):
        scratch = staging + [line_scratch(chunks - tail), pltpu.VMEM(price_shape, F32)]
        if final:
            shape = (like(hours, gens), like(hours, stores), like(hours, lines))
            out_specs = (vmem(), vmem(), hbm())
        else:
            shape = (like(hours, units), like(hours, 1)) + step_out
            scratch += flow_scratch(chunks // 2 - 1)
            out_specs = (vmem(),) * len(shape)
        return pl.pallas_call(
            functools.partial(step_kernel, chunks, quarter_tiles, balance_step, final),
            out_shape=shape,
            in_specs=lists + [vmem()] * (11 + (chunks - tail) // 2 + final),
            out_specs=out_specs,
            scratch_shapes=scratch,
            compiler_params=params(STEP_MIB),
            name="step",
            cost_estimate=cost(4),
        )

    spans = [1 << b for b in reversed(range(years.bit_length() - 1))]
    order = [0]
    for bit in spans:
        order += [j ^ bit for j in order]

    def hourly_call(final):
        shape = (like(hours, units),)
        if not final:
            shape += (like(hours + 8, units), like(groups, 8, stores))
        return pl.pallas_call(
            functools.partial(hourly_kernel, years, hours, order, final),
            out_shape=shape,
            in_specs=[smem()] + [vmem()] * (6 + years),
            out_specs=(vmem(),) * len(shape),
            scratch_shapes=[
                pltpu.VMEM((years, sent_rows, stores), F32),
                pltpu.VMEM((hours + 16, units), F32),
                pltpu.VMEM((groups, 8, stores), F32),
                pltpu.VMEM((groups, 8, stores), F32),
                pltpu.VMEM((hours, stores), F32),
            ],
            compiler_params=params(STEP_MIB),
            name="hourly",
            cost_estimate=cost(2.4),
        )

    def swap(x, bit, axis="bus"):
        size = lax.axis_size(axis)
        return lax.ppermute(x, axis, [(i, i ^ bit) for i in range(size)])

    def hear(stacked, over):
        for bit in over:
            stacked = jnp.concatenate([stacked, swap(stacked, bit, "tm")])
        return stacked

    bits = [1 << b for b in range(chunks.bit_length() - 1)]
    near_dual = jnp.zeros((hours, lines), F32)
    far_dual = jnp.zeros((hours, lines), F32)
    ramp_dual = jnp.zeros((hours + 8, units), F32)
    state_dual = jnp.zeros((groups, 8, stores), F32)
    balance_dual = jnp.zeros((hours, 1), F32)
    compact, spill, base, load_sum, state, unit_rows, *made = first_call(
        few, ents, pars, sorted_bus, load, ptdf_tiles, place, gen_start, charge_start, mine_row
    )
    held = (few, ents, compact, spill)
    half_way = chunks // 2

    def renew(dual, flows, from_line):
        limits = SIGMA * lax.dynamic_slice(flow_limit, (from_line,), (lines,))
        shift = dual + SIGMA * flows
        after = shift - jnp.clip(shift, -limits, limits)
        return after, (2.0 * after - dual).astype(BF16)

    for iteration in range(ITERS):
        final = iteration == ITERS - 1
        *made, balance, picked = made
        made = [lower_call(*held, base, picked, balance), *made]
        sums = [x.astype(F32) for x in made]
        for bit in bits[:-1]:
            for d in range(half_way):
                if d & bit and not d & (bit - 1):
                    sums[d ^ bit] = sums[d ^ bit] + swap(sums[d].astype(BF16), bit).astype(F32)
        ready = sums[0].astype(BF16)
        got = swap(ready, half_way)
        if iteration == 0:
            whole_list, state, ready = lax.optimization_barrier((few, state, ready))
            turned = turn_call(whole_list, compact)
        else:
            state, ready = lax.optimization_barrier((state, ready))
        heard = hear(hours_call(state, back)[None], spans)
        fixed, *duals = hourly_call(final)(
            where, state, unit_rows, pars, place, ramp_dual, state_dual,
            *[heard[j] for j in range(years)],
        )
        if iteration == 0:
            got, fixed, turned = lax.optimization_barrier((got, fixed, turned))
        else:
            got, fixed = lax.optimization_barrier((got, fixed))
        ours, theirs = ready.astype(F32), got.astype(F32)
        balances = ours[:, lines : lines + LANE] + theirs[:, lines : lines + LANE]
        near_dual, near = renew(
            near_dual, ours[:, :lines] + theirs[:, lines + LANE :], near_line
        )
        far_dual, far = renew(far_dual, ours[:, lines + LANE :] + theirs[:, :lines], far_line)
        have = {0: jnp.concatenate([near, far], axis=1)}
        for bit in reversed(bits[:-1]):
            for d in list(have):
                have[d | bit] = swap(have[d], bit)
        bars = [have[d] for d in range(half_way)]
        prices = price_call(0, tail, True)(*held, turned, bars[0])
        made = step_call(final)(
            *held, turned, prices, state, fixed, balance_dual, balances, unit_rows, base, load_sum, back,
            mine_row, *bars[1:], *([near_dual] if final else []),
        )
        if not final:
            ramp_dual, state_dual = duals
            state, balance_dual, *made = made
    return made


STEP_MIB = 16
SPILL = 1500


def solution(mesh):
    rows = P(("scen", "tm"), "bus")
    return jax.shard_map(
        shards,
        mesh=mesh,
        in_specs=(rows, rows, rows, P("bus", None, None)) + (P("bus"),) * 10 + (P(),),
        out_specs=(rows, rows, rows),
        check_vma=False,
    )
```
